128 devices in a mesh: dp: 16 (over x_hi, z, core), tensor: 8 (over y, x_lo).
Axes of the slice: x: 4 (x_hi: 2, x_lo: 2; x = x_hi * 2 + x_lo), y: 4, z: 4, core: 2. Of those that a mesh axis runs over, the one named last changes fastest.
Arguments:
- hidden_in: bfloat16 [32, 96, 8192], P('dp', 'tensor'), may hold values from -40 to 40
- norm_gain: float32 [8192], replicated, may hold values from 0.5 to 1.5
- w_query: bfloat16 [8192, 4096], P(None, 'tensor'), may hold values from -1.41421356 to 1.41421356
- w_key: bfloat16 [8192, 1024], P(None, 'tensor'), may hold values from -0.044194174 to 0.044194174
- w_value: bfloat16 [8192, 1024], P(None, 'tensor'), may hold values from -0.0625 to 0.0625
- w_out: bfloat16 [4096, 8192], P('tensor'), may hold values from -0.09375 to 0.09375
- cotangent: bfloat16 [32, 96, 8192], P('dp', 'tensor'), may hold values from -6 to 6
Outputs:
- layer_out: bfloat16 [32, 96, 8192], P('dp', 'tensor')
- input_grad: bfloat16 [32, 96, 8192], P('dp', 'tensor')
- query_grad: float32 [8192, 4096], P('dp', 'tensor')
- key_grad: float32 [8192, 1024], P('dp', 'tensor')
- value_grad: float32 [8192, 1024], P('dp', 'tensor')
- out_grad: float32 [4096, 8192], P('tensor', 'dp')
- gain_grad: float32 [8192], P(('dp', 'tensor'))
The draws below stay inside these ranges and needn't reach their ends.
All inputs are finite; a program needn't handle non-finite values.
Results may differ from the reference program's by a relative error of at most 0.035.
Values may be sent and summed in bfloat16 or wider, within the bound.
A program may use at most 256 MiB of HBM per device.

```python
import math
import jax
import jax.numpy as jnp
from jax import lax

D = 8192
HEADS = 32
KVH = 8
HD = 128
SEQ = 96
SEQS = 32
N_DP = 16
N_TENSOR = 8


def shared_keys(key):
    return jnp.clip(jax.random.normal(key, (D, KVH * HD), jnp.float32), -4.0, 4.0)


def draw_w_key(key, part):
    key_base = shared_keys(key)
    return (key_base * D ** (-0.5)).astype(jnp.bfloat16)


def draw_w_query(key, part):
    key = jax.random.fold_in(key, 5)
    noise_key = jax.random.fold_in(key, 0)
    own_draw = jnp.clip(jax.random.normal(noise_key, (D, HEADS * HD), jnp.float32), -4.0, 4.0)
    return (own_draw * D ** (-0.5)).astype(jnp.bfloat16)


def draw_hidden_in(key, part):
    key = jax.random.fold_in(key, 7)
    noise_key, row_key, col_key = jax.random.split(key, 3)
    row_scale = jnp.exp(jax.random.uniform(row_key, (SEQS, SEQ, 1), jnp.float32, math.log(0.3), math.log(3.0)))
    col_scale = jnp.exp(jax.random.uniform(col_key, (1, 1, D), jnp.float32, math.log(0.3), math.log(3.0)))
    noise_draw = jnp.clip(jax.random.normal(noise_key, (SEQS, SEQ, D), jnp.float32), -4.0, 4.0)
    return (noise_draw * row_scale * col_scale).astype(jnp.bfloat16)


def spiked(result, key, source, target, shards_of, factor):
    def block_of(position):
        return (jnp.arange(result.shape[position]) // (result.shape[position] // shards_of)).reshape((-1,) + (1,) * (result.ndim - 1 - position))

    one_side = jax.random.permutation(key, shards_of)[block_of(target)]
    far = (block_of(target) + shards_of // 2) % shards_of
    return jnp.where((block_of(source) == one_side) | (block_of(source) == far), factor * result, result)


def levels(own_key, extent, cuts, low, top_value):
    level, own = 1.0, jax.random.fold_in(own_key, 6)
    for dim, shards_of in cuts:
        draws = jnp.exp(jax.random.uniform(jax.random.fold_in(own, dim), (shards_of,), jnp.float32, low / len(cuts), top_value / len(cuts)))
        level = level * jnp.repeat(draws, extent[dim] // shards_of).reshape([-1 if axis == dim else 1 for axis in range(len(extent))])
    return level


def noise(own_key, dims, deviation, bound, cuts=(), kind=jnp.bfloat16):
    level = levels(own_key, dims, cuts, -0.22, 0.18) if cuts else 1.0
    drawn = jax.random.normal(own_key, dims, jnp.float32) * deviation * level
    return jnp.minimum(jnp.maximum(drawn, -bound), bound).astype(kind)


def bell_draw_with(stream_key, extent, scale, reach, cuts, heavy, kind=jnp.bfloat16):
    array = scale * jax.random.normal(stream_key, extent, jnp.float32)
    if cuts:
        array = array * levels(stream_key, extent, cuts, -0.22, 0.18)
    return jnp.clip(spiked(array, jax.random.fold_in(stream_key, 3), *heavy), -reach, reach).astype(kind)


def setup_inputs(seed: int = 0) -> dict:
    seeds = jax.random.split(jax.random.key(seed), 8)
    return {
        "hidden_in": draw_hidden_in(jax.random.fold_in(seeds[7], 71), 0),
        "norm_gain": jnp.clip(1.0 + 0.1 * jax.random.normal(seeds[1], (D,), jnp.float32), 0.5, 1.5),
        "w_query": draw_w_query(jax.random.fold_in(seeds[7], 71), 0),
        "w_key": draw_w_key(jax.random.fold_in(seeds[7], 71), 0),
        "w_value": noise(seeds[4], (D, KVH * HD), D ** -0.5, 0.0625, ((1, 8),)),
        "w_out": noise(seeds[5], (HEADS * HD, D), (HEADS * HD) ** -0.5, 0.09375, ((0, 8),)),
        "cotangent": bell_draw_with(seeds[6], (SEQS, SEQ, D), 1.0, 6.0, ((0, 16), (1, 8)), (0, 2, 16, 2.0)),
    }


EPS = 1e-05
ROPE_BASE = 10000.0

def rope_tables(length, head_width):
    half_width = head_width // 2
    frequency = ROPE_BASE ** (-2.0 * jnp.arange(half_width, dtype=jnp.float32) / head_width)
    angles = jnp.arange(length, dtype=jnp.float32)[:, None] * frequency[None, :]
    cosine_table = jnp.concatenate([jnp.cos(angles), jnp.cos(angles)], axis=1)
    sine_table = jnp.concatenate([jnp.sin(angles), jnp.sin(angles)], axis=1)
    return (cosine_table, sine_table)

def rotate(vectors, cosine_table, sine_table):
    half_width = vectors.shape[-1] // 2
    turned = jnp.concatenate([-vectors[..., half_width:], vectors[..., :half_width]], axis=-1)
    return vectors * cosine_table[:, None, :] + turned * sine_table[:, None, :]

def unrotate(gradient, cosine_table, sine_table):
    half_width = gradient.shape[-1] // 2
    scaled = gradient * sine_table[:, None, :]
    rotated_back = jnp.concatenate([scaled[..., half_width:], -scaled[..., :half_width]], axis=-1)
    return gradient * cosine_table[:, None, :] + rotated_back

def attention_weights(query_rot, key_rot):
    seq_count, length, head_count, head_width = query_rot.shape
    key_heads = key_rot.shape[2]
    grouped = query_rot.reshape(seq_count, length, key_heads, head_count // key_heads, head_width)
    logits = jnp.einsum('bqgjd,bkgd->bgjqk', grouped.astype(jnp.float32), key_rot.astype(jnp.float32)) * head_width ** (-0.5)
    rows_at = lax.broadcasted_iota(jnp.int32, (length, length), 0)
    cols_at = lax.broadcasted_iota(jnp.int32, (length, length), 1)
    logits = jnp.where(rows_at >= cols_at, logits, -1e+30)
    largest = lax.optimization_barrier(jnp.max(logits, axis=-1, keepdims=True))
    powers = jnp.exp(logits - largest)
    return powers / lax.optimization_barrier(jnp.sum(powers, axis=-1, keepdims=True))

def attention_mix(attn_probs, values):
    weights = attn_probs.astype(jnp.bfloat16)
    seq_count, key_heads, per_group, length, _ = weights.shape
    mixed_heads = jnp.einsum('bgjqk,bkgd->bqgjd', weights.astype(jnp.float32), values.astype(jnp.float32))
    return mixed_heads.reshape(seq_count, length, key_heads * per_group * values.shape[-1]).astype(jnp.bfloat16)

def attention_grads(query_rot, key_rot, values, grad_mixed):
    seq_count, length, head_count, head_width = query_rot.shape
    key_heads = key_rot.shape[2]
    per_group = head_count // key_heads
    attn_probs = attention_weights(query_rot, key_rot)
    weights = attn_probs.astype(jnp.bfloat16).astype(jnp.float32)
    grouped_grad = grad_mixed.reshape(seq_count, length, key_heads, per_group, head_width).astype(jnp.float32)
    grouped_query = query_rot.reshape(seq_count, length, key_heads, per_group, head_width).astype(jnp.float32)
    dvalues = jnp.einsum('bgjqk,bqgjd->bkgd', weights, grouped_grad)
    prob_grad = jnp.einsum('bqgjd,bkgd->bgjqk', grouped_grad, values.astype(jnp.float32))
    row_delta = lax.optimization_barrier(jnp.sum(attn_probs * prob_grad, axis=-1, keepdims=True))
    score_grad = (attn_probs * (prob_grad - row_delta) * head_width ** (-0.5)).astype(jnp.bfloat16).astype(jnp.float32)
    dquery_rot = jnp.einsum('bgjqk,bkgd->bqgjd', score_grad, key_rot.astype(jnp.float32))
    dkey_rot = jnp.einsum('bgjqk,bqgjd->bkgd', score_grad, grouped_query)
    return (dquery_rot.reshape(seq_count, length, head_count, head_width), dkey_rot, dvalues)

def rounded(term):
    return lax.optimization_barrier(term.astype(jnp.bfloat16)).astype(jnp.float32)

def reference(hidden_in, norm_gain, w_query, w_key, w_value, w_out, cotangent):
    query_cols = HEADS * HD
    key_cols = KVH * HD
    rows_group = 2 * SEQ
    cosine_table, sine_table = rope_tables(SEQ, HD)
    query_wide = w_query.astype(jnp.float32).reshape(D, N_TENSOR, query_cols // N_TENSOR)
    key_wide = w_key.astype(jnp.float32).reshape(D, N_TENSOR, key_cols // N_TENSOR)
    value_wide = w_value.astype(jnp.float32).reshape(D, N_TENSOR, key_cols // N_TENSOR)
    out_wide = w_out.astype(jnp.float32).reshape(N_TENSOR, query_cols // N_TENSOR, D)
    inputs = hidden_in.reshape(N_DP, 2, SEQ, D)
    grads_in = cotangent.reshape(N_DP, 2, SEQ, D)

    def group_step(totals, group_data):
        query_total, key_total, value_total, out_total, gain_total = totals
        row_block, grad_rows = group_data
        as_float = row_block.astype(jnp.float32)
        inverse = lax.rsqrt(lax.optimization_barrier(jnp.mean(as_float * as_float, axis=-1, keepdims=True)) + EPS)
        scaled_in = as_float * inverse
        normed = (scaled_in * norm_gain).astype(jnp.bfloat16)
        flat_normed = normed.reshape(rows_group, D)
        query_pre = jnp.dot(flat_normed, w_query, preferred_element_type=jnp.float32).reshape(2, SEQ, HEADS, HD)
        key_pre = jnp.dot(flat_normed, w_key, preferred_element_type=jnp.float32).reshape(2, SEQ, KVH, HD)
        value_pre = jnp.dot(flat_normed, w_value, preferred_element_type=jnp.float32).reshape(2, SEQ, KVH, HD)
        query_rot = rotate(query_pre, cosine_table, sine_table).astype(jnp.bfloat16)
        key_rot = rotate(key_pre, cosine_table, sine_table).astype(jnp.bfloat16)
        values = value_pre.astype(jnp.bfloat16)
        mixed_heads = attention_mix(attention_weights(query_rot, key_rot), values)
        flat_mixed = mixed_heads.reshape(rows_group, query_cols)
        split_mixed = flat_mixed.astype(jnp.float32).reshape(rows_group, N_TENSOR, query_cols // N_TENSOR)
        projected = lax.optimization_barrier(jnp.sum(rounded(jnp.einsum('rtk,tkd->trd', split_mixed, out_wide)), axis=0))
        layer_out = (as_float + projected.reshape(2, SEQ, D)).astype(jnp.bfloat16)
        flat_grad = grad_rows.reshape(rows_group, D)
        out_total = out_total + rounded(jnp.dot(flat_mixed.T, flat_grad, preferred_element_type=jnp.float32))
        grad_mixed = jnp.dot(flat_grad, w_out.T, preferred_element_type=jnp.float32).astype(jnp.bfloat16)
        dquery_rot, dkey_rot, dvalues = attention_grads(query_rot, key_rot, values, grad_mixed.reshape(2, SEQ, HEADS, HD))
        grad_query = unrotate(dquery_rot, cosine_table, sine_table).astype(jnp.bfloat16).reshape(rows_group, query_cols)
        grad_key = unrotate(dkey_rot, cosine_table, sine_table).astype(jnp.bfloat16).reshape(rows_group, key_cols)
        grad_value = dvalues.astype(jnp.bfloat16).reshape(rows_group, key_cols)
        query_total = query_total + rounded(jnp.dot(flat_normed.T, grad_query, preferred_element_type=jnp.float32))
        key_total = key_total + rounded(jnp.dot(flat_normed.T, grad_key, preferred_element_type=jnp.float32))
        value_total = value_total + rounded(jnp.dot(flat_normed.T, grad_value, preferred_element_type=jnp.float32))
        normed_terms = jnp.einsum('rtk,dtk->trd', grad_query.astype(jnp.float32).reshape(rows_group, N_TENSOR, -1), query_wide)
        normed_terms = normed_terms + jnp.einsum('rtk,dtk->trd', grad_key.astype(jnp.float32).reshape(rows_group, N_TENSOR, -1), key_wide)
        normed_terms = normed_terms + jnp.einsum('rtk,dtk->trd', grad_value.astype(jnp.float32).reshape(rows_group, N_TENSOR, -1), value_wide)
        normed_grad = lax.optimization_barrier(jnp.sum(rounded(normed_terms), axis=0)).reshape(2, SEQ, D)
        weighted = normed_grad * norm_gain
        input_grad = grad_rows.astype(jnp.float32) + inverse * (weighted - scaled_in * lax.optimization_barrier(jnp.mean(weighted * scaled_in, axis=-1, keepdims=True)))
        gain_total = gain_total + lax.optimization_barrier(jnp.sum(normed_grad * scaled_in, axis=(0, 1)))
        return ((query_total, key_total, value_total, out_total, gain_total), (layer_out, input_grad.astype(jnp.bfloat16)))
    start_totals = (jnp.zeros((D, query_cols), jnp.float32), jnp.zeros((D, key_cols), jnp.float32), jnp.zeros((D, key_cols), jnp.float32), jnp.zeros((query_cols, D), jnp.float32), jnp.zeros((D,), jnp.float32))
    totals, stacked = lax.scan(group_step, start_totals, (inputs, grads_in))
    query_total, key_total, value_total, out_total, gain_total = totals
    layer_out, input_grad = stacked
    return (layer_out.reshape(SEQS, SEQ, D), input_grad.reshape(SEQS, SEQ, D), query_total, key_total, value_total, out_total, gain_total)
```

```python
import functools

import jax
import jax.numpy as jnp
from jax import lax
from jax.experimental import pallas as pl
from jax.experimental.pallas import tpu as pltpu
from jax.sharding import PartitionSpec as P

HD = 128
EPS = 1e-05
ROPE_BASE = 10000.0
NEG = -1e30
BF, F32 = jnp.bfloat16, jnp.float32
SLOTS, ROWS, D = 8, 24, 8192
HALF = D // 2
TOK = SLOTS * ROWS
PIECES, PIECE, SLICE = 5, 256, 512
MESH_ID = pl.DeviceIdType.MESH


def place():
    dp, tensor = lax.axis_index("dp"), lax.axis_index("tensor")
    core, chip = lax.rem(dp, 2), dp // 2
    z, xh = lax.rem(chip, 4), chip // 4
    y, xl = tensor // 2, lax.rem(tensor, 2)
    here = dict(z=z, xh=xh, core=core, y=y, xl=xl, dp=dp, tensor=tensor)

    def along_z(at):
        return ((xh * 4 + at) * 2 + core, tensor)

    def along_y(at):
        return (dp, at * 2 + xl)

    here["z_up"] = along_z(lax.rem(z + 1, 4))
    here["z_down"] = along_z(lax.rem(z + 3, 4))
    here["y_up"] = along_y(lax.rem(y + 1, 4))
    here["y_down"] = along_y(lax.rem(y + 3, 4))
    here["x_lo"] = (dp, y * 2 + 1 - xl)
    here["x_hi"] = (((1 - xh) * 4 + z) * 2 + core, tensor)
    here["sibling"] = (chip * 2 + 1 - core, tensor)
    here["z_even"] = along_z(z + 1 - 2 * lax.rem(z, 2))
    here["z_odd"] = along_z(3 - z)
    here["y_even"] = along_y(y + 1 - 2 * lax.rem(y, 2))
    here["y_odd"] = along_y(3 - y)
    return here


def greet(devices):
    barrier = pltpu.get_barrier_semaphore()
    for device in devices:
        pl.semaphore_signal(barrier, inc=1, device_id=device, device_id_type=MESH_ID)
    pl.semaphore_wait(barrier, len(devices))


def remote(src, dst, send, recv, device):
    return pltpu.make_async_remote_copy(
        src_ref=src, dst_ref=dst, send_sem=send, recv_sem=recv, device_id=device, device_id_type=MESH_ID
    )


def gather_kernel(first, second, first_all, second_all, first_sib, second_sib, send, recv, sib_send, sib_recv, local):
    here = place()
    y, xl, core = here["y"], here["xl"], here["core"]
    up, down = lax.rem(y + 1, 4), lax.rem(y + 3, 4)
    far = lax.rem(y + 2, 4)
    own, mate = here["tensor"], y * 2 + 1 - xl
    greet([here["y_up"], here["y_down"], here["x_lo"], here["sibling"]])
    arrays = ((first, first_all, first_sib), (second, second_all, second_sib))
    started = []

    def push(a, number, slot, device, src=None):
        whole = arrays[a][1]
        copy = remote(whole.at[slot] if src is None else src, whole.at[slot], send.at[a, number], recv.at[a, slot], device)
        copy.start()
        started.append(copy)

    def landed(a, slot):
        whole = arrays[a][1]
        remote(whole.at[slot], whole.at[slot], send.at[a, 0], recv.at[a, slot], here["x_lo"]).wait_recv()

    def share(a, number, slot, src=None):
        _, whole, sib = arrays[a]
        copy = remote(
            whole.at[slot, 1 - core] if src is None else src.at[1 - core],
            sib.at[slot], sib_send.at[a, number], sib_recv.at[a, slot], here["sibling"],
        )
        copy.start()
        started.append(copy)

    keep = []
    for a in range(2):
        src, whole, _ = arrays[a]
        push(a, 0, own, here["x_lo"], src)
        push(a, 1, own, here["y_up"], src)
        push(a, 2, own, here["y_down"], src)
        copy = pltpu.make_async_copy(src, whole.at[own], local.at[a])
        copy.start()
        keep.append(copy)
        share(a, 0, own, src)
    for a in range(2):
        landed(a, mate)
        push(a, 3, mate, here["y_up"])
        push(a, 4, mate, here["y_down"])
        share(a, 1, mate)
        landed(a, down * 2)
        push(a, 5, down * 2, here["y_up"])
        share(a, 2, down * 2)
        landed(a, up * 2 + 1)
        push(a, 6, up * 2 + 1, here["y_down"])
        share(a, 3, up * 2 + 1)
        landed(a, down * 2 + 1)
        share(a, 4, down * 2 + 1)
        landed(a, up * 2)
        share(a, 5, up * 2)
    for a in range(2):
        landed(a, far * 2)
        share(a, 6, far * 2)
        landed(a, far * 2 + 1)
        share(a, 7, far * 2 + 1)
    for copy in keep:
        copy.wait()
    for copy in started:
        copy.wait_send()
    for a in range(2):
        _, whole, sib = arrays[a]
        for slot in range(SLOTS):
            remote(
                whole.at[slot, 0], sib.at[slot], sib_send.at[a, 0], sib_recv.at[a, slot], here["sibling"]
            ).wait_recv()


def gather(first, second):
    whole = jax.ShapeDtypeStruct((SLOTS, 2, ROWS, HALF), BF)
    sib = jax.ShapeDtypeStruct((SLOTS, ROWS, HALF), BF)
    dma = pltpu.SemaphoreType.DMA
    return pl.pallas_call(
        gather_kernel,
        out_shape=(whole, whole, sib, sib),
        in_specs=[pl.BlockSpec(memory_space=pl.ANY)] * 2,
        out_specs=tuple([pl.BlockSpec(memory_space=pl.ANY)] * 4),
        scratch_shapes=[dma((2, 7)), dma((2, SLOTS)), dma((2, 8)), dma((2, SLOTS)), dma((2,))],
        compiler_params=pltpu.CompilerParams(collective_id=0, has_side_effects=True),
    )(first, second)


def scatter_kernel(
    part_a, part_b, turned, cot_own, cot_sib, norm_own, norm_sib, gain_in,
    out_a, out_b, out_w, out_g,
    turned_sib, far_s, side_s, near_s, pair_s, far_r, side_r, near_r, pair_r,
    t_near_s, t_pair_s, t_far_r, t_side_r, t_near_r, t_pair_r, gain_s, gain_r,
    sib_sems, w_send, w_recv, t_send, t_recv, g_send, g_recv,
):
    here = place()
    y, xl, z, xh = here["y"], here["xl"], here["z"], here["xh"]
    y_up, y_down, y_far = lax.rem(y + 1, 4), lax.rem(y + 3, 4), lax.rem(y + 2, 4)
    z_up, z_down, z_far = lax.rem(z + 1, 4), lax.rem(z + 3, 4), lax.rem(z + 2, 4)
    greet([here[name] for name in ("y_up", "y_down", "x_lo", "z_up", "z_down", "x_hi", "sibling")])
    parts, outs = (part_a, part_b), (out_a, out_b)
    toward = ((here["y_up"], y_up), (here["y_down"], y_down))
    toward_z = ((here["z_up"], z_up), (here["z_down"], z_down))

    swap = remote(turned, turned_sib, sib_sems.at[0], sib_sems.at[1], here["sibling"])
    swap.start()

    def t_copy(kind, a, way):
        device, at = toward[way]
        if kind == 0:
            src, dst = parts[a].at[y_far * 2 + way], t_far_r.at[a, way]
        elif kind == 1:
            src, dst = parts[a].at[at * 2 + 1 - way], t_side_r.at[a, way]
        elif kind == 2:
            src, dst = t_near_s.at[a, way], t_near_r.at[a, way]
        return remote(src, dst, t_send.at[kind, a, way], t_recv.at[kind, a, way], device)

    for kind in range(2):
        for a in range(2):
            for way in range(2):
                t_copy(kind, a, way).start()

    ways = ("sibling", "y_even", "y_odd", "x_lo", "z_even", "z_odd", "x_hi")

    def g_copy(step):
        return remote(gain_s.at[step], gain_r.at[step], g_send.at[step], g_recv.at[step], here[ways[step]])

    def gain_step(step):
        if step:
            g_copy(step - 1).wait()
            gain_s[step] = gain_s[step - 1] + gain_r[step - 1]
        if step < 7:
            g_copy(step).start()

    gain_s[0] = gain_in[...]
    gain_step(0)
    swap.wait()

    def product(p, chip, own, sib):
        columns = pl.ds(pl.multiple_of(chip * SLICE, SLICE), SLICE)
        total = jnp.dot(turned[p], own[:, columns], preferred_element_type=F32)
        return total + jnp.dot(turned_sib[p], sib[:, columns], preferred_element_type=F32)

    def w_copy(kind, p, way):
        device, _ = toward_z[way]
        src, dst = ((far_s, far_r), (side_s, side_r), (near_s, near_r))[kind]
        return remote(src.at[way, p], dst.at[way, p], w_send.at[kind, way, p], w_recv.at[kind, way, p], device)

    def pair_copy(p):
        return remote(pair_s.at[p], pair_r.at[p], w_send.at[3, 0, p], w_recv.at[3, 0, p], here["x_hi"])

    streams = ((0, 2, cot_own, cot_sib), (2, PIECES, norm_own, norm_sib))

    def each(body):
        for low, high, own, sib in streams:
            @pl.loop(low, high)
            def _(p, own=own, sib=sib):
                body(p, own, sib)

    def first_blocks(p, own, sib):
        for way in range(2):
            far_s[way, p] = product(p, way * 4 + z_far, own, sib).astype(BF)
            w_copy(0, p, way).start()
        for way in range(2):
            side_s[way, p] = product(p, (1 - way) * 4 + toward_z[way][1], own, sib).astype(BF)
            w_copy(1, p, way).start()

    each(first_blocks)
    gain_step(1)

    width = 1024

    def over_columns(body):
        @pl.loop(0, D // width)
        def _(i):
            body(pl.ds(pl.multiple_of(i * width, width), width))

    for a in range(2):
        for way in range(2):
            t_copy(0, a, way).wait()
            at = toward[way][1]

            def relay(columns, a=a, way=way, at=at):
                t_near_s[a, way, :, columns] = (
                    parts[a][at * 2 + way, :, columns].astype(F32) + t_far_r[a, way, :, columns].astype(F32)
                ).astype(BF)

            over_columns(relay)
            t_copy(2, a, way).start()
    gain_step(2)

    def second_blocks(p, own, sib):
        for way in range(2):
            block = product(p, way * 4 + toward_z[way][1], own, sib)
            w_copy(0, p, way).wait()
            near_s[way, p] = (block + far_r[way, p].astype(F32)).astype(BF)
            w_copy(2, p, way).start()

    each(second_blocks)
    gain_step(3)

    def t_pair(a):
        return remote(t_pair_s.at[a], t_pair_r.at[a], t_send.at[3, a, 0], t_recv.at[3, a, 0], here["x_lo"])

    def t_total(a, side, columns):
        return (
            parts[a][y * 2 + side, :, columns].astype(F32)
            + t_side_r[a, 1 - side, :, columns].astype(F32)
            + t_near_r[a, side, :, columns].astype(F32)
        )

    for a in range(2):
        for way in range(2):
            t_copy(1, a, way).wait()
            t_copy(2, a, way).wait()

        def settle(columns, a=a):
            t_pair_s[a, :, columns] = t_total(a, 1 - xl, columns).astype(BF)
            outs[a][:, columns] = t_total(a, xl, columns)

        over_columns(settle)
        t_pair(a).start()
    gain_step(4)

    def last_blocks(p, own, sib):
        for way in range(2):
            w_copy(1, p, way).wait()
            w_copy(2, p, way).wait()
        theirs, mine = 1 - xh, xh
        pair_s[p] = (
            product(p, theirs * 4 + z, own, sib)
            + side_r[1 - theirs, p].astype(F32) + near_r[theirs, p].astype(F32)
        ).astype(BF)
        pair_copy(p).start()
        out_w[p] = (
            product(p, mine * 4 + z, own, sib)
            + side_r[1 - mine, p].astype(F32) + near_r[mine, p].astype(F32)
        )

    each(last_blocks)
    gain_step(5)
    for a in range(2):
        t_pair(a).wait()

        def finish(columns, a=a):
            outs[a][:, columns] = outs[a][:, columns] + t_pair_r[a, :, columns].astype(F32)

        over_columns(finish)
    gain_step(6)

    @pl.loop(0, PIECES)
    def _(p):
        pair_copy(p).wait()
        out_w[p] = out_w[p] + pair_r[p].astype(F32)

    gain_step(7)
    out_g[...] = gain_s[7]


def scatter(part_a, part_b, turned, cot_own, cot_sib, norm_own, norm_sib, gain):
    dma = pltpu.SemaphoreType.DMA
    block = (PIECES, PIECE, SLICE)
    rows = (ROWS, D)
    return pl.pallas_call(
        scatter_kernel,
        out_shape=(
            jax.ShapeDtypeStruct(rows, F32),
            jax.ShapeDtypeStruct(rows, F32),
            jax.ShapeDtypeStruct(block, F32),
            jax.ShapeDtypeStruct((64, 128), F32),
        ),
        in_specs=[pl.BlockSpec(memory_space=pltpu.VMEM)] * 8,
        out_specs=tuple([pl.BlockSpec(memory_space=pltpu.VMEM)] * 4),
        scratch_shapes=[
            pltpu.VMEM((PIECES, PIECE, TOK), BF),
            pltpu.VMEM((2,) + block, BF), pltpu.VMEM((2,) + block, BF), pltpu.VMEM((2,) + block, BF),
            pltpu.VMEM(block, BF),
            pltpu.VMEM((2,) + block, BF), pltpu.VMEM((2,) + block, BF), pltpu.VMEM((2,) + block, BF),
            pltpu.VMEM(block, BF),
            pltpu.VMEM((2, 2) + rows, BF), pltpu.VMEM((2,) + rows, BF),
            pltpu.VMEM((2, 2) + rows, BF), pltpu.VMEM((2, 2) + rows, BF), pltpu.VMEM((2, 2) + rows, BF),
            pltpu.VMEM((2,) + rows, BF),
            pltpu.VMEM((8, 64, 128), F32), pltpu.VMEM((7, 64, 128), F32),
            dma((2,)), dma((4, 2, PIECES)), dma((4, 2, PIECES)),
            dma((4, 2, 2)), dma((4, 2, 2)), dma((7,)), dma((7,)),
        ],
        compiler_params=pltpu.CompilerParams(
            collective_id=1, has_side_effects=True, vmem_limit_bytes=60 * 1024 * 1024
        ),
    )(part_a, part_b, turned, cot_own, cot_sib, norm_own, norm_sib, gain)


def rope_tables(length, head_width):
    half_width = head_width // 2
    frequency = ROPE_BASE ** (-2.0 * jnp.arange(half_width, dtype=F32) / head_width)
    angles = jnp.arange(length, dtype=F32)[:, None] * frequency[None, :]
    cosine_table = jnp.concatenate([jnp.cos(angles), jnp.cos(angles)], axis=1)
    sine_table = jnp.concatenate([jnp.sin(angles), jnp.sin(angles)], axis=1)
    return (cosine_table, sine_table)


def rotate(vectors, cosine_table, sine_table):
    half_width = vectors.shape[-1] // 2
    turned = jnp.concatenate([-vectors[..., half_width:], vectors[..., :half_width]], axis=-1)
    return vectors * cosine_table[:, None, :] + turned * sine_table[:, None, :]


def unrotate(gradient, cosine_table, sine_table):
    half_width = gradient.shape[-1] // 2
    scaled = gradient * sine_table[:, None, :]
    rotated_back = jnp.concatenate([scaled[..., half_width:], -scaled[..., :half_width]], axis=-1)
    return gradient * cosine_table[:, None, :] + rotated_back


def dot(a, b, ca, cb):
    return lax.dot_general(a, b, (((ca,), (cb,)), ((), ())), preferred_element_type=F32)


def shards(hidden_in, norm_gain, w_query, w_key, w_value, w_out, cotangent):
    seqs, own_len, _ = hidden_in.shape
    query_cols, key_cols = w_query.shape[1], w_key.shape[1]
    heads = query_cols // HD
    core = lax.rem(lax.axis_index("dp"), 2)
    hidden = hidden_in.reshape(ROWS, D).astype(F32)
    cot = cotangent.reshape(ROWS, D)
    inverse = lax.rsqrt(jnp.mean(hidden * hidden, axis=-1, keepdims=True) + EPS)
    scaled_in = hidden * inverse
    normed = (scaled_in * norm_gain).astype(BF)

    def by_parity(rows):
        return rows.reshape(ROWS, 8, 2, SLICE).transpose(2, 0, 1, 3).reshape(2, ROWS, HALF)

    def natural(rows):
        return rows.reshape(SLOTS, 2, ROWS, 8, SLICE).transpose(0, 2, 3, 1, 4).reshape(TOK, D)

    def own_half(rows):
        return lax.dynamic_index_in_dim(rows, core, 1, keepdims=False).reshape(TOK, HALF)

    norm_all, cot_all, norm_sib, cot_sib = gather(by_parity(normed), by_parity(cot))
    norm_flat, cot_flat = natural(norm_all), natural(cot_all)

    order = jnp.arange(TOK)
    seq_of = (order // own_len) % seqs
    pos_of = (order // ROWS) * own_len + order % own_len
    cosine_table, sine_table = rope_tables(own_len * SLOTS, HD)
    cosine_table, sine_table = cosine_table[pos_of], sine_table[pos_of]
    allowed = (seq_of[:, None] == seq_of[None, :]) & (pos_of[:, None] >= pos_of[None, :])

    query = dot(norm_flat, w_query, 1, 0).reshape(TOK, heads, HD)
    key = dot(norm_flat, w_key, 1, 0).reshape(TOK, 1, HD)
    values = dot(norm_flat, w_value, 1, 0).astype(BF)
    query_rot = rotate(query, cosine_table, sine_table).astype(BF)
    key_rot = rotate(key, cosine_table, sine_table).astype(BF)[:, 0]
    logits = jnp.einsum("qhd,kd->hqk", query_rot, key_rot, preferred_element_type=F32) * HD ** (-0.5)
    logits = jnp.where(allowed[None], logits, NEG)
    powers = jnp.exp(logits - jnp.max(logits, axis=-1, keepdims=True))
    probs = powers / jnp.sum(powers, axis=-1, keepdims=True)
    weights = probs.astype(BF)
    mixed = jnp.einsum("hqk,kd->qhd", weights, values, preferred_element_type=F32).astype(BF)
    mixed_flat = mixed.reshape(TOK, query_cols)
    projected = dot(mixed_flat, w_out, 1, 0).astype(BF)

    grad_mixed = dot(cot_flat, w_out, 1, 1).astype(BF).reshape(TOK, heads, HD)
    dvalues = jnp.einsum("hqk,qhd->kd", weights, grad_mixed, preferred_element_type=F32)
    prob_grad = jnp.einsum("qhd,kd->hqk", grad_mixed, values, preferred_element_type=F32)
    row_delta = jnp.sum(probs * prob_grad, axis=-1, keepdims=True)
    score_grad = (probs * (prob_grad - row_delta) * HD ** (-0.5)).astype(BF)
    dquery = jnp.einsum("hqk,kd->qhd", score_grad, key_rot, preferred_element_type=F32)
    dkey = jnp.einsum("hqk,qhd->kd", score_grad, query_rot, preferred_element_type=F32)
    grad_query = unrotate(dquery, cosine_table, sine_table).astype(BF).reshape(TOK, query_cols)
    grad_key = unrotate(dkey[:, None], cosine_table, sine_table).astype(BF).reshape(TOK, key_cols)
    grad_value = dvalues.astype(BF)
    normed_part = (
        dot(grad_query, w_query, 1, 1) + dot(grad_key, w_key, 1, 1) + dot(grad_value, w_value, 1, 1)
    ).astype(BF)
    gain_part = jnp.sum(normed_part.astype(F32) * norm_flat.astype(F32), axis=0) / norm_gain

    columns = jnp.concatenate([mixed_flat, grad_query, grad_key, grad_value], axis=1)
    turned = columns.T.reshape(PIECES, PIECE, TOK)
    project_share, normed_grad, weight_share, gain_total = scatter(
        projected.reshape(SLOTS, ROWS, D), normed_part.reshape(SLOTS, ROWS, D), turned,
        own_half(cot_all), cot_sib.reshape(TOK, HALF), own_half(norm_all), norm_sib.reshape(TOK, HALF),
        gain_part.reshape(64, 128),
    )
    layer_out = (hidden + project_share).astype(BF).reshape(seqs, own_len, D)
    weighted = normed_grad * norm_gain
    input_grad = cot.astype(F32) + inverse * (
        weighted - scaled_in * jnp.mean(weighted * scaled_in, axis=-1, keepdims=True)
    )
    input_grad = input_grad.astype(BF).reshape(seqs, own_len, D)
    weight_share = weight_share.reshape(PIECES * PIECE, SLICE)
    out_share = weight_share[:query_cols]
    joint_share = weight_share[query_cols:].T
    share = D // 128
    at = lax.axis_index("dp") * 8 + lax.axis_index("tensor")
    gain_share = lax.dynamic_slice_in_dim(gain_total.reshape(D), at * share, share, 0)
    return (
        layer_out, input_grad, joint_share[:, :query_cols], joint_share[:, query_cols : query_cols + key_cols],
        joint_share[:, query_cols + key_cols :], out_share, gain_share,
    )


def solution(mesh):
    return jax.shard_map(
        shards,
        mesh=mesh,
        in_specs=(
            P("dp", "tensor", None), P(), P(None, "tensor"), P(None, "tensor"), P(None, "tensor"),
            P("tensor", None), P("dp", "tensor", None),
        ),
        out_specs=(
            P("dp", "tensor", None), P("dp", "tensor", None), P("dp", "tensor"), P("dp", "tensor"),
            P("dp", "tensor"), P("tensor", "dp"), P(("dp", "tensor")),
        ),
        check_vma=False,
    )
```

```python
import jax
import jax.numpy as jnp
import numpy as np
from jax import lax
from jax.experimental import pallas as pl
from jax.experimental.pallas import tpu as pltpu
from jax.sharding import PartitionSpec as P

HD = 128
EPS = 1e-05
ROPE_BASE = 10000.0
BF, F32 = jnp.bfloat16, jnp.float32
SLOTS, ROWS, D = 8, 24, 8192
PAIR, HALF = 2 * ROWS, D // 2
TOK = SLOTS * ROWS
SEQ_ROWS = 12
HEADS = 4
QC, KC = 512, 128
PIECES, PIECE, SLICE = 5, 256, 512
SCALE = HD ** (-0.5)
MESH_ID = pl.DeviceIdType.MESH
MIB = 1024 * 1024


def place():
    dp, tensor = lax.axis_index("dp"), lax.axis_index("tensor")
    core, chip = lax.rem(dp, 2), dp // 2
    z, xh = lax.rem(chip, 4), chip // 4
    y, xl = tensor // 2, lax.rem(tensor, 2)
    here = dict(z=z, xh=xh, core=core, y=y, xl=xl, dp=dp, tensor=tensor)

    def along_z(at):
        return ((xh * 4 + at) * 2 + core, tensor)

    def along_y(at):
        return (dp, at * 2 + xl)

    here["z_up"] = along_z(lax.rem(z + 1, 4))
    here["z_down"] = along_z(lax.rem(z + 3, 4))
    here["y_up"] = along_y(lax.rem(y + 1, 4))
    here["y_down"] = along_y(lax.rem(y + 3, 4))
    here["x_lo"] = (dp, y * 2 + 1 - xl)
    here["x_hi"] = (((1 - xh) * 4 + z) * 2 + core, tensor)
    here["sibling"] = (chip * 2 + 1 - core, tensor)
    here["z_even"] = along_z(z + 1 - 2 * lax.rem(z, 2))
    here["z_odd"] = along_z(3 - z)
    here["y_even"] = along_y(y + 1 - 2 * lax.rem(y, 2))
    here["y_odd"] = along_y(3 - y)
    return here


def greet(devices):
    barrier = pltpu.get_barrier_semaphore()
    for device in devices:
        pl.semaphore_signal(barrier, inc=1, device_id=device, device_id_type=MESH_ID)
    pl.semaphore_wait(barrier, len(devices))


def remote(src, dst, send, recv, device):
    return pltpu.make_async_remote_copy(
        src_ref=src, dst_ref=dst, send_sem=send, recv_sem=recv, device_id=device, device_id_type=MESH_ID
    )


def dot(a, b, ca=1, cb=0):
    return lax.dot_general(a, b, (((ca,), (cb,)), ((), ())), preferred_element_type=F32)


def cols(at, width=SLICE):
    return pl.ds(pl.multiple_of(at * width, width), width)


def layer_kernel(
    hidden, cot, gain, w_query, w_key, w_value, w_out, cosine, sine, bias,
    layer_out, input_grad, query_share, key_share, value_share, out_share, gain_out,
    wq, wkv, wo, rows_n, rows_c, flat_n, flat_c, sib_n, sib_c, turned, turned_sib,
    t_far_r, t_side_r, t_near_r, t_pair_r, far_r, side_r, near_r, pair_r,
    gain_s, gain_r, query_acc, kv_acc, query_rot, key_rot, values, mixed, grad_mixed, grad_query, grad_kv, probs,
    inverse, summed,
    w_sems, wo_sems, a_send, a_recv, s_send, s_recv, d_send, d_recv, t_send, t_recv, g_send, g_recv,
):
    here = place()
    y, xl, z, xh, core = here["y"], here["xl"], here["z"], here["xh"], here["core"]
    y_up, y_down, y_far = lax.rem(y + 1, 4), lax.rem(y + 3, 4), lax.rem(y + 2, 4)
    z_up, z_down, z_far = lax.rem(z + 1, 4), lax.rem(z + 3, 4), lax.rem(z + 2, 4)
    own, mate = here["tensor"], y * 2 + 1 - xl
    toward = ((here["y_up"], y_up), (here["y_down"], y_down))
    toward_z = ((here["z_up"], z_up), (here["z_down"], z_down))
    rows = (rows_n, rows_c)

    loads = (
        pltpu.make_async_copy(w_query, wq, w_sems.at[0]),
        pltpu.make_async_copy(w_key, wkv.at[:, pl.ds(0, KC)], w_sems.at[1]),
        pltpu.make_async_copy(w_value, wkv.at[:, pl.ds(KC, KC)], w_sems.at[2]),
    )

    def load_out(b):
        half, block = b // 16, lax.rem(b, 16)
        return pltpu.make_async_copy(w_out.at[cols(half, PIECE), cols(block)], wo.at[b], wo_sems.at[b])

    for copy in loads:
        copy.start()

    @pl.loop(0, 32)
    def _(b):
        load_out(b).start()

    def square(i, total):
        block = hidden[:, cols(i)].astype(F32)
        return total + jnp.sum(block * block, axis=1, keepdims=True)

    mean = lax.fori_loop(0, 16, square, jnp.zeros((ROWS, 1), F32)) / D
    inverse[...] = jnp.broadcast_to(lax.rsqrt(mean + EPS), (ROWS, 128))

    @pl.loop(0, 8)
    def _(k):
        scale = inverse[:, :1]
        normed = [
            hidden[:, cols(2 * k + p)].astype(F32) * scale * gain[:, cols(2 * k + p)] for p in range(2)
        ]
        rows_n[own, :, cols(k)] = jnp.concatenate(normed, axis=0).astype(BF)
        rows_c[own, :, cols(k)] = jnp.concatenate(
            [cot[:, cols(2 * k + p)].astype(F32) for p in range(2)], axis=0
        ).astype(BF)

    greet([here[name] for name in ("y_up", "y_down", "x_lo", "z_up", "z_down", "x_hi", "sibling")])

    pushed = ([], [])

    def push(a, number, slot, device):
        copy = remote(rows[a].at[slot], rows[a].at[slot], a_send.at[a, number], a_recv.at[a, slot], device)
        copy.start()
        pushed[a].append(copy)

    def landed(a, slot):
        remote(rows[a].at[slot], rows[a].at[slot], a_send.at[a, 0], a_recv.at[a, slot], here["x_lo"]).wait_recv()

    def push_own(a):
        push(a, 0, own, here["x_lo"])
        push(a, 1, own, here["y_up"])
        push(a, 2, own, here["y_down"])

    def push_mate(a):
        landed(a, mate)
        push(a, 3, mate, here["y_up"])
        push(a, 4, mate, here["y_down"])

    def push_far(a):
        landed(a, y_down * 2)
        push(a, 5, y_down * 2, here["y_up"])
        landed(a, y_up * 2 + 1)
        push(a, 6, y_up * 2 + 1, here["y_down"])

    def rest(a):
        landed(a, y_down * 2 + 1)
        landed(a, y_up * 2)
        landed(a, y_far * 2)
        landed(a, y_far * 2 + 1)

    def flatten(a, k):
        chunks = [rows[a][slot, :, cols(k)].astype(F32) for slot in range(SLOTS)]
        return [
            jnp.concatenate([c[p * ROWS : (p + 1) * ROWS] for c in chunks], axis=0).astype(BF) for p in range(2)
        ]

    def to_sibling(number, src, dst):
        return remote(src, dst, s_send.at[number], s_recv.at[number], here["sibling"])

    push_own(0)
    push_mate(0)
    push_far(0)
    push_own(1)
    rest(0)

    query_acc[...] = jnp.zeros_like(query_acc)
    kv_acc[...] = jnp.zeros_like(kv_acc)
    for copy in loads:
        copy.wait()

    @pl.loop(0, 8)
    def _(k):
        for p, block in enumerate(flatten(0, k)):
            flat_n[p, :, cols(k)] = block
            query_acc[...] += dot(block, wq[cols(2 * k + p), :])
            kv_acc[...] += dot(block, wkv[cols(2 * k + p), :])

    share_n = to_sibling(0, flat_n.at[1 - core], sib_n)
    share_n.start()
    push_mate(1)

    def rotated(u):
        return u * cosine[...] + pltpu.roll(u, HD // 2, 1) * sine[...]

    def unrotated(g):
        return g * cosine[...] - pltpu.roll(g, HD // 2, 1) * sine[...]

    def head(h):
        return slice(h * HD, (h + 1) * HD)

    key_rot[...] = rotated(kv_acc[:, :HD]).astype(BF)
    values[...] = kv_acc[:, HD:].astype(BF)
    for h in range(HEADS):
        query_rot[:, head(h)] = rotated(query_acc[:, head(h)]).astype(BF)
    for h in range(HEADS):
        logits = dot(query_rot[:, head(h)], key_rot[...], 1, 1) * SCALE + bias[...]
        powers = jnp.exp(logits - jnp.max(logits, axis=1, keepdims=True))
        prob = powers / jnp.sum(powers, axis=1, keepdims=True)
        probs[h] = prob
        mixed[:, head(h)] = dot(prob.astype(BF), values[...]).astype(BF)
    push_far(1)
    for p in range(2):
        turned[p] = mixed[:, p * PIECE : (p + 1) * PIECE].astype(F32).T.astype(BF)
    share_mixed = to_sibling(1, turned.at[pl.ds(0, 2)], turned_sib.at[pl.ds(0, 2)])
    share_mixed.start()

    @pl.loop(0, 32)
    def _(b):
        load_out(b).wait()

    for copy in pushed[0]:
        copy.wait_send()

    def to_chunks(a, k, blocks):
        for slot in range(SLOTS):
            rows[a][slot, :, cols(k)] = jnp.concatenate(
                [b[slot * ROWS : (slot + 1) * ROWS] for b in blocks], axis=0
            ).astype(BF)

    @pl.loop(0, 8)
    def _(k):
        to_chunks(0, k, [
            dot(mixed[:, :PIECE], wo[2 * k + p]) + dot(mixed[:, PIECE:], wo[16 + 2 * k + p]) for p in range(2)
        ])

    def t_copy(kind, a, way):
        device, at = toward[way]
        slot = (y_far * 2 + way, at * 2 + 1 - way, at * 2 + way)[kind]
        dst = (t_far_r, t_side_r, t_near_r)[kind].at[a, way]
        return remote(rows[a].at[slot], dst, t_send.at[kind, a, way], t_recv.at[kind, a, way], device)

    def t_start(a):
        for kind in range(2):
            for way in range(2):
                t_copy(kind, a, way).start()

    def t_relay(a):
        for way in range(2):
            t_copy(0, a, way).wait()
            slot = toward[way][1] * 2 + way

            @pl.loop(0, 8)
            def _(k, way=way, slot=slot):
                rows[a][slot, :, cols(k)] = (
                    rows[a][slot, :, cols(k)].astype(F32) + t_far_r[a, way, :, cols(k)].astype(F32)
                ).astype(BF)

            t_copy(2, a, way).start()

    def t_total(a, side, k):
        return (
            rows[a][y * 2 + side, :, cols(k)].astype(F32)
            + t_side_r[a, 1 - side, :, cols(k)].astype(F32)
            + t_near_r[a, side, :, cols(k)].astype(F32)
        )

    def t_pair(a):
        return remote(rows[a].at[mate], t_pair_r.at[a], t_send.at[3, a, 0], t_recv.at[3, a, 0], here["x_lo"])

    def t_settle(a):
        for way in range(2):
            t_copy(1, a, way).wait()
            t_copy(2, a, way).wait()

        @pl.loop(0, 8)
        def _(k):
            rows[a][mate, :, cols(k)] = t_total(a, 1 - xl, k).astype(BF)

        t_pair(a).start()

    rest(1)
    t_start(0)

    query_acc[...] = jnp.zeros_like(query_acc)

    @pl.loop(0, 8)
    def _(k):
        for p, block in enumerate(flatten(1, k)):
            flat_c[p, :, cols(k)] = block
            for half in range(2):
                query_acc[:, half * PIECE : (half + 1) * PIECE] += dot(block, wo[half * 16 + 2 * k + p], 1, 1)

    share_c = to_sibling(2, flat_c.at[1 - core], sib_c)
    share_c.start()
    grad_mixed[...] = query_acc[...].astype(BF)

    def product(p, chip, flat, sib):
        total = dot(turned[p], flat[core, :, cols(chip)])
        return total + dot(turned_sib[p], sib[:, cols(chip)])

    def stage(kind, p, way):
        return (kind * 2 + way) * PIECES + p

    def d_copy(kind, p, way):
        device, _ = toward_z[way]
        dst = (far_r, side_r, near_r)[kind].at[way, p]
        return remote(wo.at[stage(kind, p, way)], dst, d_send.at[kind, way, p], d_recv.at[kind, way, p], device)

    def d_pair(p):
        return remote(wo.at[stage(0, p, 0)], pair_r.at[p], d_send.at[3, 0, p], d_recv.at[3, 0, p], here["x_hi"])

    def first_blocks(low, high, flat, sib):
        @pl.loop(low, high)
        def _(p):
            for way in range(2):
                wo[stage(0, p, way)] = product(p, way * 4 + z_far, flat, sib).astype(BF)
                d_copy(0, p, way).start()
            for way in range(2):
                wo[stage(1, p, way)] = product(p, (1 - way) * 4 + toward_z[way][1], flat, sib).astype(BF)
                d_copy(1, p, way).start()

    def second_blocks(low, high, flat, sib):
        @pl.loop(low, high)
        def _(p):
            for way in range(2):
                block = product(p, way * 4 + toward_z[way][1], flat, sib)
                d_copy(0, p, way).wait()
                wo[stage(2, p, way)] = (block + far_r[way, p].astype(F32)).astype(BF)
                d_copy(2, p, way).start()

    def d_total(p, side, flat, sib):
        return (
            product(p, side * 4 + z, flat, sib)
            + side_r[1 - side, p].astype(F32) + near_r[side, p].astype(F32)
        )

    def third_blocks(low, high, flat, sib):
        @pl.loop(low, high)
        def _(p):
            for way in range(2):
                d_copy(1, p, way).wait()
                d_copy(2, p, way).wait()
            wo[stage(0, p, 0)] = d_total(p, 1 - xh, flat, sib).astype(BF)
            d_pair(p).start()

    share_mixed.wait()
    share_c.wait()
    first_blocks(0, 2, flat_c, sib_c)
    t_relay(0)

    dkey = jnp.zeros((TOK, HD), F32)
    dvalues = jnp.zeros((TOK, HD), F32)
    for h in range(HEADS):
        prob = probs[h]
        grad = grad_mixed[:, head(h)]
        dvalues += dot(prob.astype(BF), grad, 0, 0)
        prob_grad = dot(grad, values[...], 1, 1)
        row_delta = jnp.sum(prob * prob_grad, axis=1, keepdims=True)
        score_grad = (prob * (prob_grad - row_delta) * SCALE).astype(BF)
        grad_query[:, head(h)] = unrotated(dot(score_grad, key_rot[...])).astype(BF)
        dkey += dot(score_grad, query_rot[:, head(h)], 0, 0)
    grad_kv[:, :HD] = unrotated(dkey).astype(BF)
    grad_kv[:, HD:] = dvalues.astype(BF)
    for p in range(2):
        turned[2 + p] = grad_query[:, p * PIECE : (p + 1) * PIECE].astype(F32).T.astype(BF)
    turned[4] = grad_kv[...].astype(F32).T.astype(BF)
    share_grads = to_sibling(3, turned.at[pl.ds(2, 3)], turned_sib.at[pl.ds(2, 3)])
    share_grads.start()
    share_n.wait()
    share_grads.wait()
    first_blocks(2, PIECES, flat_n, sib_n)

    for copy in pushed[1]:
        copy.wait_send()

    @pl.loop(0, 8)
    def _(k):
        blocks = []
        for p in range(2):
            at = 2 * k + p
            block = dot(grad_query[...], wq[cols(at), :], 1, 1) + dot(grad_kv[...], wkv[cols(at), :], 1, 1)
            blocks.append(block)
            terms = block.astype(BF).astype(F32) * flat_n[p, :, cols(k)].astype(F32)
            gain_s[0, pl.ds(at, 1), :] = jnp.sum(terms, axis=0, keepdims=True) / gain[:, cols(at)]
        to_chunks(1, k, blocks)

    t_start(1)

    ways = ("sibling", "y_even", "y_odd", "x_lo", "z_even", "z_odd", "x_hi")

    def g_copy(step):
        return remote(gain_s.at[step], gain_r.at[step], g_send.at[step], g_recv.at[step], here[ways[step]])

    def gain_step(step):
        if step:
            g_copy(step - 1).wait()
            gain_s[step] = gain_s[step - 1] + gain_r[step - 1]
        if step < 7:
            g_copy(step).start()

    gain_step(0)
    second_blocks(0, 2, flat_c, sib_c)
    gain_step(1)
    t_settle(0)
    second_blocks(2, PIECES, flat_n, sib_n)
    gain_step(2)
    t_relay(1)
    gain_step(3)
    third_blocks(0, 2, flat_c, sib_c)
    gain_step(4)
    t_settle(1)
    t_pair(0).wait()

    @pl.loop(0, 8)
    def _(k):
        total = t_total(0, xl, k) + t_pair_r[0, :, cols(k)].astype(F32)
        for p in range(2):
            at = cols(2 * k + p)
            layer_out[:, at] = (hidden[:, at].astype(F32) + total[p * ROWS : (p + 1) * ROWS]).astype(BF)

    gain_step(5)
    third_blocks(2, PIECES, flat_n, sib_n)
    gain_step(6)
    t_pair(1).wait()
    scale = inverse[:, :1]

    def weigh(k, total):
        block = t_total(1, xl, k) + t_pair_r[1, :, cols(k)].astype(F32)
        summed[:, cols(k)] = block
        for p in range(2):
            at = cols(2 * k + p)
            scaled = hidden[:, at].astype(F32) * scale
            weighted = block[p * ROWS : (p + 1) * ROWS] * gain[:, at]
            total = total + jnp.sum(weighted * scaled, axis=1, keepdims=True)
        return total

    mean = lax.fori_loop(0, 8, weigh, jnp.zeros((ROWS, 1), F32)) / D

    @pl.loop(0, 8)
    def _(k):
        block = summed[:, cols(k)]
        for p in range(2):
            at = cols(2 * k + p)
            scaled = hidden[:, at].astype(F32) * scale
            weighted = block[p * ROWS : (p + 1) * ROWS] * gain[:, at]
            input_grad[:, at] = (cot[:, at].astype(F32) + scale * (weighted - scaled * mean)).astype(BF)

    gain_step(7)
    gain_out[...] = gain_s[7]

    def final(p, flat, sib):
        total = d_total(p, xh, flat, sib)
        d_pair(p).wait()
        return total + pair_r[p].astype(F32)

    for p in range(2):
        out_share[p * PIECE : (p + 1) * PIECE, :] = final(p, flat_c, sib_c)
    for p in range(2):
        query_share[:, p * PIECE : (p + 1) * PIECE] = final(2 + p, flat_n, sib_n).T
    both = final(4, flat_n, sib_n)
    key_share[...] = both[:KC].T
    value_share[...] = both[KC:].T


def tables(own_len):
    token = np.arange(TOK)
    seq = (token // own_len) % 2
    pos = (token // ROWS) * own_len + token % own_len
    frequency = ROPE_BASE ** (-2.0 * np.arange(HD // 2) / HD)
    angles = pos[:, None] * frequency[None, :]
    cosine = np.concatenate([np.cos(angles), np.cos(angles)], axis=1).astype(np.float32)
    sine = np.concatenate([-np.sin(angles), np.sin(angles)], axis=1).astype(np.float32)
    allowed = (seq[:, None] == seq[None, :]) & (pos[:, None] >= pos[None, :])
    return cosine, sine, np.where(allowed, 0.0, -1e30).astype(np.float32)


def shards(hidden_in, norm_gain, w_query, w_key, w_value, w_out, cotangent):
    dma, vmem = pltpu.SemaphoreType.DMA, pltpu.VMEM
    chunk = (PAIR, HALF)
    block = (PIECE, SLICE)
    at_vmem = pl.BlockSpec(memory_space=pltpu.VMEM)
    at_any = pl.BlockSpec(memory_space=pl.ANY)
    shape = jax.ShapeDtypeStruct
    cosine, sine, bias = tables(SEQ_ROWS)
    layer_out, input_grad, query_share, key_share, value_share, out_share, gain_total = pl.pallas_call(
        layer_kernel,
        out_shape=(
            shape((ROWS, D), BF), shape((ROWS, D), BF), shape((SLICE, QC), F32), shape((SLICE, KC), F32),
            shape((SLICE, KC), F32), shape((QC, SLICE), F32), shape((16, SLICE), F32),
        ),
        in_specs=[at_vmem] * 3 + [at_any] * 4 + [at_vmem] * 3,
        out_specs=tuple([at_vmem] * 7),
        scratch_shapes=[
            vmem((D, QC), BF), vmem((D, 2 * KC), BF), vmem((32,) + block, BF),
            vmem((SLOTS,) + chunk, BF), vmem((SLOTS,) + chunk, BF),
            vmem((2, TOK, HALF), BF), vmem((2, TOK, HALF), BF), vmem((TOK, HALF), BF), vmem((TOK, HALF), BF),
            vmem((PIECES, PIECE, TOK), BF), vmem((PIECES, PIECE, TOK), BF),
            vmem((2, 2) + chunk, BF), vmem((2, 2) + chunk, BF), vmem((2, 2) + chunk, BF), vmem((2,) + chunk, BF),
            vmem((2, PIECES) + block, BF), vmem((2, PIECES) + block, BF), vmem((2, PIECES) + block, BF),
            vmem((PIECES,) + block, BF),
            vmem((8, 16, SLICE), F32), vmem((7, 16, SLICE), F32),
            vmem((TOK, QC), F32), vmem((TOK, 2 * KC), F32),
            vmem((TOK, QC), BF), vmem((TOK, HD), BF), vmem((TOK, HD), BF),
            vmem((TOK, QC), BF), vmem((TOK, QC), BF), vmem((TOK, QC), BF), vmem((TOK, 2 * KC), BF),
            vmem((HEADS, TOK, TOK), F32), vmem((ROWS, 128), F32), vmem(chunk, F32),
            dma((3,)), dma((32,)), dma((2, 7)), dma((2, SLOTS)), dma((4,)), dma((4,)),
            dma((4, 2, PIECES)), dma((4, 2, PIECES)), dma((4, 2, 2)), dma((4, 2, 2)), dma((7,)), dma((7,)),
        ],
        compiler_params=pltpu.CompilerParams(
            collective_id=0, has_side_effects=True, vmem_limit_bytes=61 * MIB
        ),
    )(
        hidden_in.reshape(ROWS, D), cotangent.reshape(ROWS, D), norm_gain.reshape(1, D),
        w_query, w_key, w_value, w_out, jnp.asarray(cosine), jnp.asarray(sine), jnp.asarray(bias),
    )
    share = D // 128
    at = lax.axis_index("dp") * 8 + lax.axis_index("tensor")
    gain_share = lax.dynamic_slice_in_dim(gain_total.reshape(D), at * share, share, 0)
    return (
        layer_out.reshape(hidden_in.shape), input_grad.reshape(hidden_in.shape),
        query_share, key_share, value_share, out_share, gain_share,
    )


def solution(mesh):
    return jax.shard_map(
        shards,
        mesh=mesh,
        in_specs=(
            P("dp", "tensor", None), P(), P(None, "tensor"), P(None, "tensor"), P(None, "tensor"),
            P("tensor", None), P("dp", "tensor", None),
        ),
        out_specs=(
            P("dp", "tensor", None), P("dp", "tensor", None), P("dp", "tensor"), P("dp", "tensor"),
            P("dp", "tensor"), P("tensor", "dp"), P(("dp", "tensor")),
        ),
        check_vma=False,
    )
```

```python
import jax
import jax.numpy as jnp
import numpy as np
from jax import lax
from jax.experimental import pallas as pl
from jax.experimental.pallas import tpu as pltpu
from jax.sharding import PartitionSpec as P

HD = 128
EPS = 1e-05
ROPE_BASE = 10000.0
BF, F32 = jnp.bfloat16, jnp.float32
SLOTS, ROWS, D = 8, 24, 8192
PAIR, HALF = 2 * ROWS, D // 2
TOK = SLOTS * ROWS
SEQ_ROWS = 12
HEADS = 4
QC, KC = 512, 128
PIECES, PIECE, SLICE = 5, 256, 512
SCALE = HD ** (-0.5)
MESH_ID = pl.DeviceIdType.MESH
MIB = 1024 * 1024


def place():
    dp, tensor = lax.axis_index("dp"), lax.axis_index("tensor")
    core, chip = lax.rem(dp, 2), dp // 2
    z, xh = lax.rem(chip, 4), chip // 4
    y, xl = tensor // 2, lax.rem(tensor, 2)
    here = dict(z=z, xh=xh, core=core, y=y, xl=xl, dp=dp, tensor=tensor)

    def along_z(at, cross=0):
        return ((xh * 4 + at) * 2 + lax.rem(core + cross, 2), tensor)

    def along_y(at):
        return (dp, at * 2 + xl)

    here["z_up"] = along_z(lax.rem(z + 1, 4))
    here["z_down"] = along_z(lax.rem(z + 3, 4))
    here["z_up_cross"] = along_z(lax.rem(z + 1, 4), 1)
    here["z_down_cross"] = along_z(lax.rem(z + 3, 4), 1)
    here["pass_from"] = lax.rem(z + 3 + 2 * core, 4)
    here["pass_to"] = along_z(lax.rem(z + 1 + 2 * core, 4))
    here["y_up"] = along_y(lax.rem(y + 1, 4))
    here["y_down"] = along_y(lax.rem(y + 3, 4))
    here["x_lo"] = (dp, y * 2 + 1 - xl)
    here["x_hi"] = (((1 - xh) * 4 + z) * 2 + core, tensor)
    here["x_hi_cross"] = (((1 - xh) * 4 + z) * 2 + 1 - core, tensor)
    here["sibling"] = (chip * 2 + 1 - core, tensor)
    here["z_even"] = along_z(z + 1 - 2 * lax.rem(z, 2))
    here["z_odd"] = along_z(3 - z)
    here["y_even"] = along_y(y + 1 - 2 * lax.rem(y, 2))
    here["y_odd"] = along_y(3 - y)
    return here


def greet(devices):
    barrier = pltpu.get_barrier_semaphore()
    for device in devices:
        pl.semaphore_signal(barrier, inc=1, device_id=device, device_id_type=MESH_ID)
    pl.semaphore_wait(barrier, len(devices))


def remote(src, dst, send, recv, device):
    return pltpu.make_async_remote_copy(
        src_ref=src, dst_ref=dst, send_sem=send, recv_sem=recv, device_id=device, device_id_type=MESH_ID
    )


def dot(a, b, ca=1, cb=0):
    return lax.dot_general(a, b, (((ca,), (cb,)), ((), ())), preferred_element_type=F32)


def cols(at, width=SLICE):
    return pl.ds(pl.multiple_of(at * width, width), width)


def layer_kernel(
    hidden, cot, gain, w_query, w_key, w_value, w_out, cosine, sine, bias,
    layer_out, input_grad, query_share, key_share, value_share, out_share, gain_out,
    wq, wkv, wo, rows_n, rows_c, flat_n, flat_c, got_n, got_c, passed, mixed, grads,
    t_far_r, t_side_r, t_near_r, t_pair_r, far_r, side_r, near_r, pair_r,
    gain_s, gain_r, query_acc, kv_acc, query_rot, key_rot, values, grad_mixed, probs,
    inverse, summed,
    w_sems, wo_sems, a_send, a_recv, f_recv, s_send, s_recv, p_recv, own_sems, c_send, c_recv, h_send, h_recv, m_send, m_recv,
    d_send, d_recv, j_send, j_recv, t_send, t_recv, g_send, g_recv,
):
    here = place()
    y, xl, z, xh, core = here["y"], here["xl"], here["z"], here["xh"], here["core"]
    y_up, y_down, y_far = lax.rem(y + 1, 4), lax.rem(y + 3, 4), lax.rem(y + 2, 4)
    z_up, z_down, z_far = lax.rem(z + 1, 4), lax.rem(z + 3, 4), lax.rem(z + 2, 4)
    own, mate = here["tensor"], y * 2 + 1 - xl
    toward = ((here["y_up"], y_up), (here["y_down"], y_down))
    toward_z = ((here["z_up"], z_up), (here["z_down"], z_down))
    rows = (rows_n, rows_c)

    loads = (
        pltpu.make_async_copy(w_query, wq, w_sems.at[0]),
        pltpu.make_async_copy(w_key, wkv.at[:, pl.ds(0, KC)], w_sems.at[1]),
        pltpu.make_async_copy(w_value, wkv.at[:, pl.ds(KC, KC)], w_sems.at[2]),
    )

    def load_out(b):
        half, block = b // 16, lax.rem(b, 16)
        return pltpu.make_async_copy(w_out.at[cols(half, PIECE), cols(block)], wo.at[b], wo_sems.at[b])

    for copy in loads:
        copy.start()

    @pl.loop(0, 32)
    def _(b):
        load_out(b).start()

    def mine(ref, at):
        return ref[:, at].astype(F32)

    def give(ref, at, block):
        ref[:, at] = block.astype(BF)

    def square(i, total):
        block = mine(hidden, cols(i))
        return total + jnp.sum(block * block, axis=1, keepdims=True)

    mean = lax.fori_loop(0, 16, square, jnp.zeros((ROWS, 1), F32)) / D
    inverse[...] = jnp.broadcast_to(lax.rsqrt(mean + EPS), (ROWS, 128))

    @pl.loop(0, 8)
    def _(k):
        scale = inverse[:, :1]
        normed = [
            mine(hidden, cols(2 * k + p)) * scale * gain[:, cols(2 * k + p)] for p in range(2)
        ]
        rows_n[own, :, cols(k)] = jnp.concatenate(normed, axis=0).astype(BF)
        rows_c[own, :, cols(k)] = jnp.concatenate(
            [mine(cot, cols(2 * k + p)) for p in range(2)], axis=0
        ).astype(BF)

    greet([here[name] for name in (
        "y_up", "y_down", "x_lo", "z_up", "z_down", "z_up_cross", "z_down_cross", "x_hi", "x_hi_cross", "sibling",
    )])

    pushed = ([], [])

    def push(a, number, slot, device):
        copy = remote(rows[a].at[slot], rows[a].at[slot], a_send.at[a, number], a_recv.at[a, slot], device)
        copy.start()
        pushed[a].append(copy)

    def landed(a, slot):
        remote(rows[a].at[slot], rows[a].at[slot], a_send.at[a, 0], a_recv.at[a, slot], here["x_lo"]).wait_recv()

    def push_own(a):
        push(a, 0, own, here["x_lo"])
        push(a, 1, own, here["y_up"])
        push(a, 2, own, here["y_down"])

    def push_mate(a):
        landed(a, mate)
        push(a, 3, mate, here["y_up"])
        push(a, 4, mate, here["y_down"])

    halves = (pl.ds(0, HALF // 2), pl.ds(HALF // 2, HALF // 2))

    def far_copy(a, way):
        slot = (y_down, y_up)[way] * 2 + xl
        ref = rows[a].at[slot, :, halves[way]]
        return remote(ref, ref, a_send.at[a, 5 + way], f_recv.at[a, way], toward[way][0])

    def push_far(a):
        for way in range(2):
            landed(a, (y_down, y_up)[way] * 2 + xl)
            copy = far_copy(a, way)
            copy.start()
            pushed[a].append(copy)

    def push_last(a):
        slot = y_far * 2 + xl
        for way in range(2):
            ref = rows[a].at[slot, :, halves[way]]
            remote(ref, ref, a_send.at[a, 0], f_recv.at[a, way], here["x_lo"]).wait_recv()
        push(a, 7, slot, here["x_lo"])

    def rest(a):
        landed(a, y_down * 2 + 1 - xl)
        landed(a, y_up * 2 + 1 - xl)
        landed(a, y_far * 2 + 1 - xl)

    def flatten(a, k):
        chunks = [rows[a][slot, :, cols(k)].astype(F32) for slot in range(SLOTS)]
        return [
            jnp.concatenate([c[p * ROWS : (p + 1) * ROWS] for c in chunks], axis=0).astype(BF) for p in range(2)
        ]

    def slice_copy(number):
        cross = 1 - core
        src, dst, recv, device = (
            (flat_n.at[core, z_far], passed.at[0], p_recv.at[0], "z_up"),
            (flat_n.at[cross, z_far], passed.at[1], p_recv.at[1], "z_down"),
            (flat_n.at[core, z_up], got_n.at[z, core], s_recv.at[z, core], "z_up"),
            (flat_n.at[core, z_down], got_n.at[z, core], s_recv.at[z, core], "z_down"),
            (flat_n.at[cross, z_up], got_n.at[z, core], s_recv.at[z, core], "z_up_cross"),
            (flat_n.at[cross, z_down], got_n.at[z, core], s_recv.at[z, core], "z_down_cross"),
            (flat_n.at[cross, z], got_n.at[z, core], s_recv.at[z, core], "sibling"),
            (passed.at[0], got_n.at[z_down, core], s_recv.at[z_down, core], "z_up"),
            (passed.at[1], got_n.at[z_up, core], s_recv.at[z_up, core], "z_down_cross"),
        )[number]
        return remote(src, dst, s_send.at[number], recv, here[device])

    def own_slice():
        return pltpu.make_async_copy(flat_n.at[core, z], got_n.at[z, core], own_sems.at[0])

    def slices_start():
        for number in range(7):
            slice_copy(number).start()
        own_slice().start()

    def slices_pass():
        for number in range(2):
            slice_copy(number).wait_recv()
            slice_copy(7 + number).start()

    def slices_wait():
        own_slice().wait()
        for at, cross in ((0, 1), (1, 0), (1, 1), (2, 0), (2, 1), (3, 0), (3, 1)):
            zs, cs = lax.rem(z + at, 4), lax.rem(core + cross, 2)
            ref = got_n.at[zs, cs]
            remote(ref, ref, s_send.at[0], s_recv.at[zs, cs], here["sibling"]).wait_recv()

    def cot_copy(number):
        cross = 1 - core
        src, device = (
            (flat_c.at[core, 1 - xh], "x_hi"), (flat_c.at[cross, 1 - xh], "x_hi_cross"),
            (flat_c.at[cross, xh], "sibling"),
        )[number]
        return remote(src, got_c.at[xh, core], c_send.at[number], c_recv.at[xh, core], here[device])

    def own_cot():
        return pltpu.make_async_copy(flat_c.at[core, xh], got_c.at[xh, core], own_sems.at[1])

    def mix_copy(number):
        device = ("x_hi", "x_hi_cross", "sibling")[number]
        ref = mixed.at[xh, core]
        return remote(ref, ref, h_send.at[number], h_recv.at[xh, core], here[device])

    def cross_wait():
        own_cot().wait()
        for xs, cs in ((xh, 1 - core), (1 - xh, core), (1 - xh, 1 - core)):
            ref = got_c.at[xs, cs]
            remote(ref, ref, c_send.at[0], c_recv.at[xs, cs], here["sibling"]).wait_recv()
            ref = mixed.at[xs, cs]
            remote(ref, ref, h_send.at[0], h_recv.at[xs, cs], here["sibling"]).wait_recv()

    def columns_copy(number):
        at, device = (
            (z, "sibling"), (z, "z_up"), (z, "z_down"), (z_down, "sibling"), (z_up, "sibling"),
            (here["pass_from"], "pass_to"), (z_far, "sibling"),
        )[number]
        ref = grads.at[at, core]
        return remote(ref, ref, m_send.at[number], m_recv.at[at, core], here[device])

    def columns_got(zs, cs):
        ref = grads.at[zs, cs]
        remote(ref, ref, m_send.at[0], m_recv.at[zs, cs], here["sibling"]).wait_recv()

    def columns_start():
        for number in (1, 2, 0):
            columns_copy(number).start()

    def columns_pass():
        columns_got(z_down, core)
        columns_got(z_up, core)
        for number in (5, 3, 4):
            columns_copy(number).start()

    def columns_last():
        columns_got(z_far, core)
        columns_copy(6).start()

    def columns_wait():
        for zs in range(4):
            columns_got(zs, 1 - core)

    push_own(0)
    push_mate(0)
    push_far(0)
    push_own(1)
    push_last(0)
    rest(0)

    query_acc[...] = jnp.zeros_like(query_acc)
    kv_acc[...] = jnp.zeros_like(kv_acc)
    for copy in loads:
        copy.wait()

    @pl.loop(0, 8)
    def _(k):
        for p, block in enumerate(flatten(0, k)):
            flat_n[p, lax.rem(k, 4), k // 4] = block
            query_acc[...] += dot(block, wq[cols(2 * k + p), :])
            kv_acc[...] += dot(block, wkv[cols(2 * k + p), :])

    slices_start()
    push_mate(1)

    def rotated(u):
        return u * cosine[...] + pltpu.roll(u, HD // 2, 1) * sine[...]

    def unrotated(g):
        return g * cosine[...] - pltpu.roll(g, HD // 2, 1) * sine[...]

    def head(h):
        return slice(h * HD, (h + 1) * HD)

    key_rot[...] = rotated(kv_acc[:, :HD]).astype(BF)
    values[...] = kv_acc[:, HD:].astype(BF)
    for h in range(HEADS):
        query_rot[:, head(h)] = rotated(query_acc[:, head(h)]).astype(BF)
    for h in range(HEADS):
        logits = dot(query_rot[:, head(h)], key_rot[...], 1, 1) * SCALE + bias[...]
        powers = jnp.exp(logits - jnp.max(logits, axis=1, keepdims=True))
        prob = powers / jnp.sum(powers, axis=1, keepdims=True)
        probs[h] = prob
        mixed[xh, core, :, head(h)] = dot(prob.astype(BF), values[...]).astype(BF)
    push_far(1)
    for number in range(3):
        mix_copy(number).start()

    @pl.loop(0, 32)
    def _(b):
        load_out(b).wait()

    for copy in pushed[0]:
        copy.wait_send()

    def to_chunks(a, k, blocks):
        for slot in range(SLOTS):
            rows[a][slot, :, cols(k)] = jnp.concatenate(
                [b[slot * ROWS : (slot + 1) * ROWS] for b in blocks], axis=0
            ).astype(BF)

    @pl.loop(0, 8)
    def _(k):
        to_chunks(0, k, [
            dot(mixed[xh, core, :, :PIECE], wo[2 * k + p]) + dot(mixed[xh, core, :, PIECE:], wo[16 + 2 * k + p]) for p in range(2)
        ])

    def t_copy(kind, a, way):
        device, at = toward[way]
        slot = (y_far * 2 + way, at * 2 + 1 - way, at * 2 + way)[kind]
        dst = (t_far_r, t_side_r, t_near_r)[kind].at[a, way]
        return remote(rows[a].at[slot], dst, t_send.at[kind, a, way], t_recv.at[kind, a, way], device)

    def t_start(a):
        for kind in range(2):
            for way in range(2):
                t_copy(kind, a, way).start()

    def t_relay(a):
        for way in range(2):
            t_copy(0, a, way).wait()
            slot = toward[way][1] * 2 + way

            @pl.loop(0, 8)
            def _(k, way=way, slot=slot):
                rows[a][slot, :, cols(k)] = (
                    rows[a][slot, :, cols(k)].astype(F32) + t_far_r[a, way, :, cols(k)].astype(F32)
                ).astype(BF)

            t_copy(2, a, way).start()

    def t_total(a, side, k):
        return (
            rows[a][y * 2 + side, :, cols(k)].astype(F32)
            + t_side_r[a, 1 - side, :, cols(k)].astype(F32)
            + t_near_r[a, side, :, cols(k)].astype(F32)
        )

    def t_pair(a):
        return remote(rows[a].at[mate], t_pair_r.at[a], t_send.at[3, a, 0], t_recv.at[3, a, 0], here["x_lo"])

    def t_settle(a):
        for way in range(2):
            t_copy(1, a, way).wait()
            t_copy(2, a, way).wait()

        @pl.loop(0, 8)
        def _(k):
            rows[a][mate, :, cols(k)] = t_total(a, 1 - xl, k).astype(BF)

        t_pair(a).start()

    push_last(1)
    t_start(0)
    rest(1)

    query_acc[...] = jnp.zeros_like(query_acc)

    @pl.loop(0, 8)
    def _(k):
        for p, block in enumerate(flatten(1, k)):
            flat_c[p, k // 4, lax.rem(k, 4)] = block
            for half in range(2):
                query_acc[:, half * PIECE : (half + 1) * PIECE] += dot(block, wo[half * 16 + 2 * k + p], 1, 1)

    for number in range(3):
        cot_copy(number).start()
    own_cot().start()
    slices_pass()
    grad_mixed[...] = query_acc[...].astype(BF)

    def joint(p, side):
        total = jnp.zeros((PIECE, SLICE), F32)
        for zs in range(4):
            for cs in range(2):
                total += dot(grads[zs, cs, :, p * PIECE : (p + 1) * PIECE], got_n[zs, cs, side], 0, 0)
        return total

    def joint_pair(p):
        return remote(wo.at[p], pair_r.at[p], j_send.at[p], j_recv.at[p], here["x_hi"])

    def outer(p, at):
        total = jnp.zeros((PIECE, SLICE), F32)
        for xs in range(2):
            for cs in range(2):
                total += dot(mixed[xs, cs, :, p * PIECE : (p + 1) * PIECE], got_c[xs, cs, at], 0, 0)
        return total

    def d_copy(kind, way):
        dst = (far_r, side_r, near_r)[kind].at[way]
        return remote(wo.at[3 + kind * 2 + way], dst, d_send.at[kind, way], d_recv.at[kind, way], toward_z[way][0])

    t_relay(0)

    dkey = jnp.zeros((TOK, HD), F32)
    dvalues = jnp.zeros((TOK, HD), F32)
    for h in range(HEADS):
        prob = probs[h]
        grad = grad_mixed[:, head(h)]
        dvalues += dot(prob.astype(BF), grad, 0, 0)
        prob_grad = dot(grad, values[...], 1, 1)
        row_delta = jnp.sum(prob * prob_grad, axis=1, keepdims=True)
        score_grad = (prob * (prob_grad - row_delta) * SCALE).astype(BF)
        grads[z, core, :, head(h)] = unrotated(dot(score_grad, key_rot[...])).astype(BF)
        dkey += dot(score_grad, query_rot[:, head(h)], 0, 0)
    grads[z, core, :, QC : QC + HD] = unrotated(dkey).astype(BF)
    grads[z, core, :, QC + HD :] = dvalues.astype(BF)
    columns_start()

    for copy in pushed[1]:
        copy.wait_send()

    @pl.loop(0, 8)
    def _(k):
        blocks = []
        for p in range(2):
            at = 2 * k + p
            block = dot(grads[z, core, :, :QC], wq[cols(at), :], 1, 1)
            block += dot(grads[z, core, :, QC:], wkv[cols(at), :], 1, 1)
            blocks.append(block)
            terms = block.astype(BF).astype(F32) * flat_n[p, lax.rem(k, 4), k // 4].astype(F32)
            gain_s[0, pl.ds(at, 1), :] = jnp.sum(terms, axis=0, keepdims=True) / gain[:, cols(at)]
        to_chunks(1, k, blocks)

    t_start(1)

    ways = ("sibling", "y_even", "y_odd", "x_lo", "z_even", "z_odd", "x_hi")

    def g_copy(step):
        return remote(gain_s.at[step], gain_r.at[step], g_send.at[step], g_recv.at[step], here[ways[step]])

    def gain_step(step):
        if step:
            g_copy(step - 1).wait()
            gain_s[step] = gain_s[step - 1] + gain_r[step - 1]
        if step < 7:
            g_copy(step).start()

    gain_step(0)
    columns_pass()
    cross_wait()
    for way in range(2):
        wo[3 + way] = outer(way, z_far).astype(BF)
        d_copy(0, way).start()
    for way in range(2):
        wo[5 + way] = outer(1 - way, toward_z[way][1]).astype(BF)
        d_copy(1, way).start()
    gain_step(1)
    t_settle(0)
    columns_last()
    t_relay(1)
    gain_step(2)
    for way in range(2):
        block = outer(way, toward_z[way][1])
        d_copy(0, way).wait()
        wo[7 + way] = (block + far_r[way].astype(F32)).astype(BF)
        d_copy(2, way).start()
    slices_wait()
    columns_wait()
    for p in range(3):
        wo[p] = joint(p, 1 - xh).astype(BF)
        joint_pair(p).start()
    gain_step(3)
    t_settle(1)
    gain_step(4)
    t_pair(0).wait()

    @pl.loop(0, 8)
    def _(k):
        total = t_total(0, xl, k) + t_pair_r[0, :, cols(k)].astype(F32)
        for p in range(2):
            at = cols(2 * k + p)
            give(layer_out, at, mine(hidden, at) + total[p * ROWS : (p + 1) * ROWS])

    gain_step(5)
    gain_step(6)
    t_pair(1).wait()
    scale = inverse[:, :1]

    def weigh(k, total):
        block = t_total(1, xl, k) + t_pair_r[1, :, cols(k)].astype(F32)
        summed[:, cols(k)] = block
        for p in range(2):
            at = cols(2 * k + p)
            scaled = mine(hidden, at) * scale
            weighted = block[p * ROWS : (p + 1) * ROWS] * gain[:, at]
            total = total + jnp.sum(weighted * scaled, axis=1, keepdims=True)
        return total

    mean = lax.fori_loop(0, 8, weigh, jnp.zeros((ROWS, 1), F32)) / D

    @pl.loop(0, 8)
    def _(k):
        block = summed[:, cols(k)]
        for p in range(2):
            at = cols(2 * k + p)
            scaled = mine(hidden, at) * scale
            weighted = block[p * ROWS : (p + 1) * ROWS] * gain[:, at]
            give(input_grad, at, mine(cot, at) + scale * (weighted - scaled * mean))

    gain_step(7)
    gain_out[...] = gain_s[7, pl.ds(here["dp"], 1), :]

    for p in range(2):
        total = outer(p, z)
        d_copy(1, 1 - p).wait()
        d_copy(2, p).wait()
        out_share[p * PIECE : (p + 1) * PIECE, :] = (
            total + side_r[1 - p].astype(F32) + near_r[p].astype(F32)
        )
    for p in range(3):
        total = joint(p, xh)
        joint_pair(p).wait()
        total = (total + pair_r[p].astype(F32)).T
        if p < 2:
            query_share[:, p * PIECE : (p + 1) * PIECE] = total
        else:
            key_share[...] = total[:, :KC]
            value_share[...] = total[:, KC:]
    for number in range(9):
        slice_copy(number).wait_send()
    for number in range(7):
        columns_copy(number).wait_send()
    for number in range(3):
        cot_copy(number).wait_send()
        mix_copy(number).wait_send()


def copy_kernel(*refs):
    count = len(refs) // 2
    for i in range(count):
        refs[count + i][...] = refs[i][...]


def results(arrays):
    at_vmem = pl.BlockSpec(memory_space=pltpu.VMEM)
    return pl.pallas_call(
        copy_kernel,
        out_shape=tuple(jax.ShapeDtypeStruct(a.shape, a.dtype) for a in arrays),
        in_specs=[at_vmem] * len(arrays),
        out_specs=tuple([at_vmem] * len(arrays)),
    )(*arrays)


def tables(own_len):
    token = np.arange(TOK)
    seq = token % 2
    pos = (token // ROWS) * own_len + token % ROWS // 2
    frequency = ROPE_BASE ** (-2.0 * np.arange(HD // 2) / HD)
    angles = pos[:, None] * frequency[None, :]
    cosine = np.concatenate([np.cos(angles), np.cos(angles)], axis=1).astype(np.float32)
    sine = np.concatenate([-np.sin(angles), np.sin(angles)], axis=1).astype(np.float32)
    allowed = (seq[:, None] == seq[None, :]) & (pos[:, None] >= pos[None, :])
    return cosine, sine, np.where(allowed, 0.0, -1e30).astype(np.float32)


def shards(hidden_in, norm_gain, w_query, w_key, w_value, w_out, cotangent):
    dma, vmem = pltpu.SemaphoreType.DMA, pltpu.VMEM
    chunk = (PAIR, HALF)
    block = (PIECE, SLICE)
    at_vmem = pl.BlockSpec(memory_space=pltpu.VMEM)
    at_any = pl.BlockSpec(memory_space=pl.ANY)
    shape = jax.ShapeDtypeStruct
    cosine, sine, bias = tables(SEQ_ROWS)
    own_shape = (ROWS, D)

    def rows_of(array):
        return array.transpose(1, 0, 2).reshape(ROWS, D)

    def as_given(array):
        return array.reshape(SEQ_ROWS, 2, D).transpose(1, 0, 2)

    layer_out, input_grad, query_share, key_share, value_share, out_share, gain_total = pl.pallas_call(
        layer_kernel,
        out_shape=(
            shape(own_shape, BF), shape(own_shape, BF), shape((SLICE, QC), F32), shape((SLICE, KC), F32),
            shape((SLICE, KC), F32), shape((QC, SLICE), F32), shape((1, SLICE), F32),
        ),
        in_specs=[at_vmem] * 3 + [at_any] * 4 + [at_vmem] * 3,
        out_specs=tuple([at_vmem] * 7),
        scratch_shapes=[
            vmem((D, QC), BF), vmem((D, 2 * KC), BF), vmem((32,) + block, BF),
            vmem((SLOTS,) + chunk, BF), vmem((SLOTS,) + chunk, BF),
            vmem((2, 4, 2, TOK, SLICE), BF), vmem((2, 2, 4, TOK, SLICE), BF),
            vmem((4, 2, 2, TOK, SLICE), BF), vmem((2, 2, 4, TOK, SLICE), BF),
            vmem((2, 2, TOK, SLICE), BF), vmem((2, 2, TOK, QC), BF), vmem((4, 2, TOK, QC + 2 * KC), BF),
            vmem((2, 2) + chunk, BF), vmem((2, 2) + chunk, BF), vmem((2, 2) + chunk, BF), vmem((2,) + chunk, BF),
            vmem((2,) + block, BF), vmem((2,) + block, BF), vmem((2,) + block, BF), vmem((3,) + block, BF),
            vmem((8, 16, SLICE), F32), vmem((7, 16, SLICE), F32),
            vmem((TOK, QC), F32), vmem((TOK, 2 * KC), F32),
            vmem((TOK, QC), BF), vmem((TOK, HD), BF), vmem((TOK, HD), BF),
            vmem((TOK, QC), BF),
            vmem((HEADS, TOK, TOK), F32), vmem((ROWS, 128), F32), vmem(chunk, F32),
            dma((3,)), dma((32,)), dma((2, 8)), dma((2, SLOTS)), dma((2, 2)), dma((9,)), dma((4, 2)), dma((2,)), dma((2,)),
            dma((3,)), dma((2, 2)), dma((3,)), dma((2, 2)), dma((7,)), dma((4, 2)),
            dma((3, 2)), dma((3, 2)), dma((3,)), dma((3,)), dma((4, 2, 2)), dma((4, 2, 2)), dma((7,)), dma((7,)),
        ],
        compiler_params=pltpu.CompilerParams(
            collective_id=0, has_side_effects=True, vmem_limit_bytes=62 * MIB
        ),
    )(
        rows_of(hidden_in), rows_of(cotangent), norm_gain.reshape(1, D),
        w_query, w_key, w_value, w_out, jnp.asarray(cosine), jnp.asarray(sine), jnp.asarray(bias),
    )
    share = D // 128
    gain_share = lax.dynamic_slice_in_dim(gain_total.reshape(SLICE), lax.axis_index("tensor") * share, share, 0)
    return (as_given(layer_out), as_given(input_grad)) + results(
        (query_share, key_share, value_share, out_share)
    ) + (gain_share,)


def solution(mesh):
    return jax.shard_map(
        shards,
        mesh=mesh,
        in_specs=(
            P("dp", "tensor", None), P(), P(None, "tensor"), P(None, "tensor"), P(None, "tensor"),
            P("tensor", None), P("dp", "tensor", None),
        ),
        out_specs=(
            P("dp", "tensor", None), P("dp", "tensor", None), P("dp", "tensor"), P("dp", "tensor"),
            P("dp", "tensor"), P("tensor", "dp"), P(("dp", "tensor")),
        ),
        check_vma=False,
    )
```

```python
import jax
import jax.numpy as jnp
import numpy as np
from jax import lax
from jax.experimental import pallas as pl
from jax.experimental.pallas import tpu as pltpu
from jax.sharding import PartitionSpec as P

HD = 128
EPS = 1e-05
ROPE_BASE = 10000.0
BF, F32 = jnp.bfloat16, jnp.float32
SLOTS, ROWS, D = 8, 24, 8192
PAIR, HALF = 2 * ROWS, D // 2
TOK = SLOTS * ROWS
SEQ_ROWS = 12
HEADS = 4
QC, KC = 512, 128
PIECES, PIECE, SLICE = 5, 256, 512
SCALE = HD ** (-0.5)
MESH_ID = pl.DeviceIdType.MESH
MIB = 1024 * 1024


def place():
    dp, tensor = lax.axis_index("dp"), lax.axis_index("tensor")
    core, chip = lax.rem(dp, 2), dp // 2
    z, xh = lax.rem(chip, 4), chip // 4
    y, xl = tensor // 2, lax.rem(tensor, 2)
    here = dict(z=z, xh=xh, core=core, y=y, xl=xl, dp=dp, tensor=tensor)

    def along_z(at, cross=0):
        return ((xh * 4 + at) * 2 + lax.rem(core + cross, 2), tensor)

    def along_y(at):
        return (dp, at * 2 + xl)

    here["z_up"] = along_z(lax.rem(z + 1, 4))
    here["z_down"] = along_z(lax.rem(z + 3, 4))
    here["z_up_cross"] = along_z(lax.rem(z + 1, 4), 1)
    here["z_down_cross"] = along_z(lax.rem(z + 3, 4), 1)
    here["pass_from"] = lax.rem(z + 3 + 2 * core, 4)
    here["pass_to"] = along_z(lax.rem(z + 1 + 2 * core, 4))
    here["y_up"] = along_y(lax.rem(y + 1, 4))
    here["y_down"] = along_y(lax.rem(y + 3, 4))
    here["x_lo"] = (dp, y * 2 + 1 - xl)
    here["x_hi"] = (((1 - xh) * 4 + z) * 2 + core, tensor)
    here["x_hi_cross"] = (((1 - xh) * 4 + z) * 2 + 1 - core, tensor)
    here["sibling"] = (chip * 2 + 1 - core, tensor)
    here["chip"] = chip
    here["tensor_peers"] = [(dp, lax.rem(tensor + i, 8)) for i in range(1, 8)]
    here["chip_peers"] = [(lax.rem(chip + i, 8) * 2 + core, tensor) for i in range(1, 8)]
    return here


def greet(devices):
    barrier = pltpu.get_barrier_semaphore()
    for device in devices:
        pl.semaphore_signal(barrier, inc=1, device_id=device, device_id_type=MESH_ID)
    pl.semaphore_wait(barrier, len(devices))


def remote(src, dst, send, recv, device):
    return pltpu.make_async_remote_copy(
        src_ref=src, dst_ref=dst, send_sem=send, recv_sem=recv, device_id=device, device_id_type=MESH_ID
    )


def dot(a, b, ca=1, cb=0):
    return lax.dot_general(a, b, (((ca,), (cb,)), ((), ())), preferred_element_type=F32)


def cols(at, width=SLICE):
    return pl.ds(pl.multiple_of(at * width, width), width)


def layer_kernel(
    hidden, cot, gain, w_query, w_key, w_value, w_out, cosine, sine, bias,
    layer_out, input_grad, query_share, key_share, value_share, out_share, gain_out,
    wq, wkv, wo, rows_n, rows_c, flat_n, flat_c, got_n, got_c, passed, mixed, grads,
    t_far_r, t_side_r, t_near_r, t_pair_r, far_r, side_r, near_r, pair_r,
    gain_own, gain_t, gain_c, gain_s, query_acc, kv_acc, query_rot, key_rot, values, grad_mixed, probs,
    inverse, summed, joint_own,
    w_sems, wo_sems, a_send, a_recv, f_recv, s_send, s_recv, p_recv, own_sems, c_send, c_recv, h_send, h_recv, m_send, m_recv,
    d_send, d_recv, j_send, j_recv, t_send, t_recv, g_send, g_recv,
):
    here = place()
    y, xl, z, xh, core = here["y"], here["xl"], here["z"], here["xh"], here["core"]
    y_up, y_down, y_far = lax.rem(y + 1, 4), lax.rem(y + 3, 4), lax.rem(y + 2, 4)
    z_up, z_down, z_far = lax.rem(z + 1, 4), lax.rem(z + 3, 4), lax.rem(z + 2, 4)
    own, mate = here["tensor"], y * 2 + 1 - xl
    toward = ((here["y_up"], y_up), (here["y_down"], y_down))
    toward_z = ((here["z_up"], z_up), (here["z_down"], z_down))
    rows = (rows_n, rows_c)

    loads = (
        pltpu.make_async_copy(w_query, wq, w_sems.at[0]),
        pltpu.make_async_copy(w_key, wkv.at[:, pl.ds(0, KC)], w_sems.at[1]),
        pltpu.make_async_copy(w_value, wkv.at[:, pl.ds(KC, KC)], w_sems.at[2]),
    )

    def load_out(b):
        half, block = b // 16, lax.rem(b, 16)
        return pltpu.make_async_copy(w_out.at[cols(half, PIECE), cols(block)], wo.at[b], wo_sems.at[b])

    for copy in loads:
        copy.start()

    @pl.loop(0, 32)
    def _(b):
        load_out(b).start()

    def mine(ref, at):
        return ref[:, at].astype(F32)

    def give(ref, at, block):
        ref[:, at] = block.astype(BF)

    def square(i, total):
        block = mine(hidden, cols(i))
        return total + jnp.sum(block * block, axis=1, keepdims=True)

    mean = lax.fori_loop(0, 16, square, jnp.zeros((ROWS, 1), F32)) / D
    inverse[...] = jnp.broadcast_to(lax.rsqrt(mean + EPS), (ROWS, 128))

    @pl.loop(0, 8)
    def _(k):
        scale = inverse[:, :1]
        normed = [
            mine(hidden, cols(2 * k + p)) * scale * gain[:, cols(2 * k + p)] for p in range(2)
        ]
        rows_n[own, :, cols(k)] = jnp.concatenate(normed, axis=0).astype(BF)
        rows_c[own, :, cols(k)] = jnp.concatenate(
            [mine(cot, cols(2 * k + p)) for p in range(2)], axis=0
        ).astype(BF)

    greet(
        here["tensor_peers"] + here["chip_peers"]
        + [here[name] for name in ("z_up_cross", "z_down_cross", "x_hi_cross", "sibling")]
    )

    pushed = ([], [])

    def push(a, number, slot, device):
        copy = remote(rows[a].at[slot], rows[a].at[slot], a_send.at[a, number], a_recv.at[a, slot], device)
        copy.start()
        pushed[a].append(copy)

    def landed(a, slot):
        remote(rows[a].at[slot], rows[a].at[slot], a_send.at[a, 0], a_recv.at[a, slot], here["x_lo"]).wait_recv()

    def push_over(a):
        push(a, 0, own, here["x_lo"])

    def push_along(a):
        push(a, 1, own, here["y_up"])
        push(a, 2, own, here["y_down"])

    def push_mate(a):
        landed(a, mate)
        push(a, 3, mate, here["y_up"])
        push(a, 4, mate, here["y_down"])

    halves = (pl.ds(0, HALF // 2), pl.ds(HALF // 2, HALF // 2))

    def far_copy(a, way):
        slot = (y_down, y_up)[way] * 2 + xl
        ref = rows[a].at[slot, :, halves[way]]
        return remote(ref, ref, a_send.at[a, 5 + way], f_recv.at[a, way], toward[way][0])

    def push_far(a):
        if a:
            landed(a, y_down * 2)
            push(a, 5, y_down * 2, here["y_up"])
            landed(a, y_up * 2 + 1)
            push(a, 6, y_up * 2 + 1, here["y_down"])
            return
        for way in range(2):
            landed(a, (y_down, y_up)[way] * 2 + xl)
            copy = far_copy(a, way)
            copy.start()
            pushed[a].append(copy)

    def push_last(a):
        slot = y_far * 2 + xl
        for way in range(2):
            ref = rows[a].at[slot, :, halves[way]]
            remote(ref, ref, a_send.at[a, 0], f_recv.at[a, way], here["x_lo"]).wait_recv()
        push(a, 7, slot, here["x_lo"])

    def rest(a):
        landed(a, y_down * 2 + (1 if a else 1 - xl))
        landed(a, y_up * 2 + (0 if a else 1 - xl))
        landed(a, y_far * 2 + 1 - xl)
        if a:
            landed(a, y_far * 2 + xl)

    def flatten(a, k):
        chunks = [rows[a][slot, :, cols(k)].astype(F32) for slot in range(SLOTS)]
        return [
            jnp.concatenate([c[p * ROWS : (p + 1) * ROWS] for c in chunks], axis=0).astype(BF) for p in range(2)
        ]

    def slice_copy(number):
        cross = 1 - core
        src, dst, recv, device = (
            (flat_n.at[core, z_far], passed.at[0], p_recv.at[0], "z_up"),
            (flat_n.at[cross, z_far], passed.at[1], p_recv.at[1], "z_down"),
            (flat_n.at[core, z_up], got_n.at[z, core], s_recv.at[z, core], "z_up"),
            (flat_n.at[core, z_down], got_n.at[z, core], s_recv.at[z, core], "z_down"),
            (flat_n.at[cross, z_up], got_n.at[z, core], s_recv.at[z, core], "z_up_cross"),
            (flat_n.at[cross, z_down], got_n.at[z, core], s_recv.at[z, core], "z_down_cross"),
            (flat_n.at[cross, z], got_n.at[z, core], s_recv.at[z, core], "sibling"),
            (passed.at[0], got_n.at[z_down, core], s_recv.at[z_down, core], "z_up"),
            (passed.at[1], got_n.at[z_up, core], s_recv.at[z_up, core], "z_down_cross"),
        )[number]
        return remote(src, dst, s_send.at[number], recv, here[device])

    def own_slice():
        return pltpu.make_async_copy(flat_n.at[core, z], got_n.at[z, core], own_sems.at[0])

    def slices_pass():
        for number in range(2):
            slice_copy(number).wait_recv()
            slice_copy(7 + number).start()

    def slices_wait():
        own_slice().wait()
        for at, cross in ((0, 1), (1, 0), (1, 1), (2, 0), (2, 1), (3, 0), (3, 1)):
            zs, cs = lax.rem(z + at, 4), lax.rem(core + cross, 2)
            ref = got_n.at[zs, cs]
            remote(ref, ref, s_send.at[0], s_recv.at[zs, cs], here["sibling"]).wait_recv()

    def cot_copy(number):
        cross = 1 - core
        src, device = (
            (flat_c.at[core, 1 - xh], "x_hi"), (flat_c.at[cross, 1 - xh], "x_hi_cross"),
            (flat_c.at[cross, xh], "sibling"),
        )[number]
        return remote(src, got_c.at[xh, core], c_send.at[number], c_recv.at[xh, core], here[device])

    def own_cot():
        return pltpu.make_async_copy(flat_c.at[core, xh], got_c.at[xh, core], own_sems.at[1])

    def mix_copy(number):
        device = ("x_hi", "x_hi_cross", "sibling")[number]
        ref = mixed.at[xh, core]
        return remote(ref, ref, h_send.at[number], h_recv.at[xh, core], here[device])

    def cross_wait():
        own_cot().wait()
        for xs, cs in ((xh, 1 - core), (1 - xh, core), (1 - xh, 1 - core)):
            ref = got_c.at[xs, cs]
            remote(ref, ref, c_send.at[0], c_recv.at[xs, cs], here["sibling"]).wait_recv()
            ref = mixed.at[xs, cs]
            remote(ref, ref, h_send.at[0], h_recv.at[xs, cs], here["sibling"]).wait_recv()

    def columns_copy(number):
        at, device = (
            (z, "sibling"), (z, "z_up"), (z, "z_down"), (z_down, "sibling"), (z_up, "sibling"),
            (here["pass_from"], "pass_to"), (z_far, "sibling"),
        )[number]
        ref = grads.at[at, core]
        return remote(ref, ref, m_send.at[number], m_recv.at[at, core], here[device])

    def columns_got(zs, cs):
        ref = grads.at[zs, cs]
        remote(ref, ref, m_send.at[0], m_recv.at[zs, cs], here["sibling"]).wait_recv()

    def columns_start():
        for number in (1, 2, 0):
            columns_copy(number).start()

    def columns_pass():
        columns_got(z_down, core)
        columns_got(z_up, core)
        for number in (5, 3, 4):
            columns_copy(number).start()

    def columns_last():
        columns_got(z_far, core)
        columns_copy(6).start()

    def columns_wait():
        for zs in range(4):
            columns_got(zs, 1 - core)

    push_over(0)
    push_along(0)
    push_mate(0)
    push_far(0)
    push_over(1)
    push_last(0)
    push_along(1)
    push_mate(1)
    rest(0)

    query_acc[...] = jnp.zeros_like(query_acc)
    kv_acc[...] = jnp.zeros_like(kv_acc)
    for copy in loads:
        copy.wait()

    for step, at in enumerate((z_far, z_up, z_down, z)):
        @pl.loop(0, 2)
        def _(side, at=at):
            k = side * 4 + at
            for p, block in enumerate(flatten(0, k)):
                flat_n[p, at, side] = block
                query_acc[...] += dot(block, wq[cols(2 * k + p), :])
                kv_acc[...] += dot(block, wkv[cols(2 * k + p), :])

        for number in ((0, 1), (2, 4), (3, 5), (6,))[step]:
            slice_copy(number).start()
    own_slice().start()

    def rotated(u):
        return u * cosine[...] + pltpu.roll(u, HD // 2, 1) * sine[...]

    def unrotated(g):
        return g * cosine[...] - pltpu.roll(g, HD // 2, 1) * sine[...]

    def head(h):
        return slice(h * HD, (h + 1) * HD)

    key_rot[...] = rotated(kv_acc[:, :HD]).astype(BF)
    values[...] = kv_acc[:, HD:].astype(BF)
    for h in range(HEADS):
        query_rot[:, head(h)] = rotated(query_acc[:, head(h)]).astype(BF)
    for h in range(HEADS):
        logits = dot(query_rot[:, head(h)], key_rot[...], 1, 1) * SCALE + bias[...]
        powers = jnp.exp(logits - jnp.max(logits, axis=1, keepdims=True))
        prob = powers / jnp.sum(powers, axis=1, keepdims=True)
        probs[h] = prob
        mixed[xh, core, :, head(h)] = dot(prob.astype(BF), values[...]).astype(BF)
    for number in range(3):
        mix_copy(number).start()

    @pl.loop(0, 32)
    def _(b):
        load_out(b).wait()

    for copy in pushed[0]:
        copy.wait_send()

    def to_chunks(a, k, blocks):
        for slot in range(SLOTS):
            rows[a][slot, :, cols(k)] = jnp.concatenate(
                [b[slot * ROWS : (slot + 1) * ROWS] for b in blocks], axis=0
            ).astype(BF)

    @pl.loop(0, 8)
    def _(k):
        to_chunks(0, k, [
            dot(mixed[xh, core, :, :PIECE], wo[2 * k + p]) + dot(mixed[xh, core, :, PIECE:], wo[16 + 2 * k + p]) for p in range(2)
        ])

    def t_copy(kind, a, way):
        device, at = toward[way]
        slot = (y_far * 2 + way, at * 2 + 1 - way, at * 2 + way)[kind]
        dst = (t_far_r, t_side_r, t_near_r)[kind].at[a, way]
        return remote(rows[a].at[slot], dst, t_send.at[kind, a, way], t_recv.at[kind, a, way], device)

    def t_start(a):
        for kind in range(2):
            for way in range(2):
                t_copy(kind, a, way).start()

    def t_relay(a):
        for way in range(2):
            t_copy(0, a, way).wait()
            slot = toward[way][1] * 2 + way

            @pl.loop(0, 8)
            def _(k, way=way, slot=slot):
                rows[a][slot, :, cols(k)] = (
                    rows[a][slot, :, cols(k)].astype(F32) + t_far_r[a, way, :, cols(k)].astype(F32)
                ).astype(BF)

            t_copy(2, a, way).start()

    def t_total(a, side, k):
        return (
            rows[a][y * 2 + side, :, cols(k)].astype(F32)
            + t_side_r[a, 1 - side, :, cols(k)].astype(F32)
            + t_near_r[a, side, :, cols(k)].astype(F32)
        )

    def t_pair(a):
        return remote(rows[a].at[mate], t_pair_r.at[a], t_send.at[3, a, 0], t_recv.at[3, a, 0], here["x_lo"])

    def t_settle(a):
        for way in range(2):
            t_copy(1, a, way).wait()
            t_copy(2, a, way).wait()

        @pl.loop(0, 8)
        def _(k):
            rows[a][mate, :, cols(k)] = t_total(a, 1 - xl, k).astype(BF)

        t_pair(a).start()

    push_far(1)
    t_start(0)
    slices_pass()
    rest(1)

    query_acc[...] = jnp.zeros_like(query_acc)

    for step, side in enumerate((1 - xh, xh)):
        @pl.loop(0, 4)
        def _(at, side=side):
            k = side * 4 + at
            for p, block in enumerate(flatten(1, k)):
                flat_c[p, side, at] = block
                for half in range(2):
                    query_acc[:, half * PIECE : (half + 1) * PIECE] += dot(block, wo[half * 16 + 2 * k + p], 1, 1)

        for number in ((0, 1), (2,))[step]:
            cot_copy(number).start()
    own_cot().start()
    grad_mixed[...] = query_acc[...].astype(BF)

    def joint(p, side):
        total = jnp.zeros((PIECE, SLICE), F32)
        for zs in range(4):
            for cs in range(2):
                total += dot(grads[zs, cs, :, p * PIECE : (p + 1) * PIECE], got_n[zs, cs, side], 0, 0)
        return total

    def joint_pair(p):
        return remote(wo.at[p], pair_r.at[p], j_send.at[p], j_recv.at[p], here["x_hi"])

    def outer(p, at):
        total = jnp.zeros((PIECE, SLICE), F32)
        for xs in range(2):
            for cs in range(2):
                total += dot(mixed[xs, cs, :, p * PIECE : (p + 1) * PIECE], got_c[xs, cs, at], 0, 0)
        return total

    def d_copy(kind, way):
        dst = (far_r, side_r, near_r)[kind].at[way]
        return remote(wo.at[3 + kind * 2 + way], dst, d_send.at[kind, way], d_recv.at[kind, way], toward_z[way][0])

    dkey = jnp.zeros((TOK, HD), F32)
    dvalues = jnp.zeros((TOK, HD), F32)
    for h in range(HEADS):
        prob = probs[h]
        grad = grad_mixed[:, head(h)]
        dvalues += dot(prob.astype(BF), grad, 0, 0)
        prob_grad = dot(grad, values[...], 1, 1)
        row_delta = jnp.sum(prob * prob_grad, axis=1, keepdims=True)
        score_grad = (prob * (prob_grad - row_delta) * SCALE).astype(BF)
        grads[z, core, :, head(h)] = unrotated(dot(score_grad, key_rot[...])).astype(BF)
        dkey += dot(score_grad, query_rot[:, head(h)], 0, 0)
    grads[z, core, :, QC : QC + HD] = unrotated(dkey).astype(BF)
    grads[z, core, :, QC + HD :] = dvalues.astype(BF)
    columns_start()
    t_relay(0)

    for copy in pushed[1]:
        copy.wait_send()

    @pl.loop(0, 8)
    def _(k):
        blocks = []
        for p in range(2):
            at = 2 * k + p
            block = dot(grads[z, core, :, :QC], wq[cols(at), :], 1, 1)
            block += dot(grads[z, core, :, QC:], wkv[cols(at), :], 1, 1)
            blocks.append(block)
            terms = block.astype(BF).astype(F32) * flat_n[p, lax.rem(k, 4), k // 4].astype(F32)
            term = jnp.sum(terms, axis=0, keepdims=True) / gain[:, cols(at)]
            for quarter in range(4):
                gain_own[quarter, pl.ds(at, 1), :] = term[:, quarter * 128 : (quarter + 1) * 128]
        to_chunks(1, k, blocks)

    def gain_over(number):
        at = lax.rem(own + 1 + number, 8) // 2
        return remote(
            gain_own.at[at], gain_t.at[own], g_send.at[0, number], g_recv.at[0, own], here["tensor_peers"][number]
        )

    def gain_sibling():
        return remote(gain_s.at[0], gain_s.at[1], g_send.at[1, 0], g_recv.at[1, 0], here["sibling"])

    def gain_chips(number):
        return remote(
            gain_s.at[2], gain_c.at[here["chip"]], g_send.at[2, number], g_recv.at[2, here["chip"]],
            here["chip_peers"][number],
        )

    def gain_sum(level, ref, mine, value):
        ref[mine] = value
        for i in range(1, 8):
            at = lax.rem(mine + i, 8)
            remote(ref.at[at], ref.at[at], g_send.at[level, 0], g_recv.at[level, at], here["sibling"]).wait_recv()
        total = ref[0]
        for i in range(1, 8):
            total = total + ref[i]
        return total

    for number in range(7):
        gain_over(number).start()
    t_start(1)
    columns_pass()
    t_settle(0)
    columns_last()
    t_relay(1)
    slices_wait()
    columns_wait()
    for p in range(3):
        wo[p] = joint(p, 1 - xh).astype(BF)
        joint_pair(p).start()
    gain_s[0] = gain_sum(0, gain_t, own, gain_own[y])
    gain_sibling().start()
    cross_wait()
    for way in range(2):
        wo[3 + way] = outer(way, z_far).astype(BF)
        d_copy(0, way).start()
    for way in range(2):
        wo[5 + way] = outer(1 - way, toward_z[way][1]).astype(BF)
        d_copy(1, way).start()
    gain_sibling().wait()
    gain_s[2] = gain_s[0] + gain_s[1]
    for number in range(7):
        gain_chips(number).start()
    t_settle(1)
    for way in range(2):
        block = outer(way, toward_z[way][1])
        d_copy(0, way).wait()
        wo[7 + way] = (block + far_r[way].astype(F32)).astype(BF)
        d_copy(2, way).start()
    for p in range(3):
        joint_own[p] = joint(p, xh)
    for p in range(2):
        out_share[p * PIECE : (p + 1) * PIECE, :] = outer(p, z)
    t_pair(0).wait()

    @pl.loop(0, 8)
    def _(k):
        total = t_total(0, xl, k) + t_pair_r[0, :, cols(k)].astype(F32)
        for p in range(2):
            at = cols(2 * k + p)
            give(layer_out, at, mine(hidden, at) + total[p * ROWS : (p + 1) * ROWS])

    t_pair(1).wait()
    scale = inverse[:, :1]

    def weigh(k, total):
        block = t_total(1, xl, k) + t_pair_r[1, :, cols(k)].astype(F32)
        summed[:, cols(k)] = block
        for p in range(2):
            at = cols(2 * k + p)
            scaled = mine(hidden, at) * scale
            weighted = block[p * ROWS : (p + 1) * ROWS] * gain[:, at]
            total = total + jnp.sum(weighted * scaled, axis=1, keepdims=True)
        return total

    mean = lax.fori_loop(0, 8, weigh, jnp.zeros((ROWS, 1), F32)) / D

    @pl.loop(0, 8)
    def _(k):
        block = summed[:, cols(k)]
        for p in range(2):
            at = cols(2 * k + p)
            scaled = mine(hidden, at) * scale
            weighted = block[p * ROWS : (p + 1) * ROWS] * gain[:, at]
            give(input_grad, at, mine(cot, at) + scale * (weighted - scaled * mean))


    for p in range(2):
        d_copy(1, 1 - p).wait()
        d_copy(2, p).wait()
        out_share[p * PIECE : (p + 1) * PIECE, :] += side_r[1 - p].astype(F32) + near_r[p].astype(F32)
    for p in range(3):
        joint_pair(p).wait()
        total = (joint_own[p] + pair_r[p].astype(F32)).T
        if p < 2:
            query_share[:, p * PIECE : (p + 1) * PIECE] = total
        else:
            key_share[...] = total[:, :KC]
            value_share[...] = total[:, KC:]
    gain_s[3] = gain_sum(2, gain_c, here["chip"], gain_s[2])
    gain_out[...] = gain_s[3, pl.ds(here["dp"], 1), :]
    for number in range(7):
        gain_over(number).wait_send()
        gain_chips(number).wait_send()
    for number in range(9):
        slice_copy(number).wait_send()
    for number in range(7):
        columns_copy(number).wait_send()
    for number in range(3):
        cot_copy(number).wait_send()
        mix_copy(number).wait_send()


def copy_kernel(*refs):
    count = len(refs) // 2
    for i in range(count):
        refs[count + i][...] = refs[i][...]


def results(arrays):
    at_vmem = pl.BlockSpec(memory_space=pltpu.VMEM)
    return pl.pallas_call(
        copy_kernel,
        out_shape=tuple(jax.ShapeDtypeStruct(a.shape, a.dtype) for a in arrays),
        in_specs=[at_vmem] * len(arrays),
        out_specs=tuple([at_vmem] * len(arrays)),
    )(*arrays)


def tables(own_len):
    token = np.arange(TOK)
    seq = token % 2
    pos = (token // ROWS) * own_len + token % ROWS // 2
    frequency = ROPE_BASE ** (-2.0 * np.arange(HD // 2) / HD)
    angles = pos[:, None] * frequency[None, :]
    cosine = np.concatenate([np.cos(angles), np.cos(angles)], axis=1).astype(np.float32)
    sine = np.concatenate([-np.sin(angles), np.sin(angles)], axis=1).astype(np.float32)
    allowed = (seq[:, None] == seq[None, :]) & (pos[:, None] >= pos[None, :])
    return cosine, sine, np.where(allowed, 0.0, -1e30).astype(np.float32)


def shards(hidden_in, norm_gain, w_query, w_key, w_value, w_out, cotangent):
    dma, vmem = pltpu.SemaphoreType.DMA, pltpu.VMEM
    chunk = (PAIR, HALF)
    block = (PIECE, SLICE)
    at_vmem = pl.BlockSpec(memory_space=pltpu.VMEM)
    at_any = pl.BlockSpec(memory_space=pl.ANY)
    shape = jax.ShapeDtypeStruct
    cosine, sine, bias = tables(SEQ_ROWS)
    own_shape = (ROWS, D)

    def rows_of(array):
        return array.transpose(1, 0, 2).reshape(ROWS, D)

    def as_given(array):
        return array.reshape(SEQ_ROWS, 2, D).transpose(1, 0, 2)

    layer_out, input_grad, query_share, key_share, value_share, out_share, gain_total = pl.pallas_call(
        layer_kernel,
        out_shape=(
            shape(own_shape, BF), shape(own_shape, BF), shape((SLICE, QC), F32), shape((SLICE, KC), F32),
            shape((SLICE, KC), F32), shape((QC, SLICE), F32), shape((1, 128), F32),
        ),
        in_specs=[at_vmem] * 3 + [at_any] * 4 + [at_vmem] * 3,
        out_specs=tuple([at_vmem] * 7),
        scratch_shapes=[
            vmem((D, QC), BF), vmem((D, 2 * KC), BF), vmem((32,) + block, BF),
            vmem((SLOTS,) + chunk, BF), vmem((SLOTS,) + chunk, BF),
            vmem((2, 4, 2, TOK, SLICE), BF), vmem((2, 2, 4, TOK, SLICE), BF),
            vmem((4, 2, 2, TOK, SLICE), BF), vmem((2, 2, 4, TOK, SLICE), BF),
            vmem((2, 2, TOK, SLICE), BF), vmem((2, 2, TOK, QC), BF), vmem((4, 2, TOK, QC + 2 * KC), BF),
            vmem((2, 2) + chunk, BF), vmem((2, 2) + chunk, BF), vmem((2, 2) + chunk, BF), vmem((2,) + chunk, BF),
            vmem((2,) + block, BF), vmem((2,) + block, BF), vmem((2,) + block, BF), vmem((3,) + block, BF),
            vmem((4, 16, 128), F32), vmem((8, 16, 128), F32), vmem((8, 16, 128), F32), vmem((4, 16, 128), F32),
            vmem((TOK, QC), F32), vmem((TOK, 2 * KC), F32),
            vmem((TOK, QC), BF), vmem((TOK, HD), BF), vmem((TOK, HD), BF),
            vmem((TOK, QC), BF),
            vmem((HEADS, TOK, TOK), F32), vmem((ROWS, 128), F32), vmem(chunk, F32), vmem((3,) + block, F32),
            dma((3,)), dma((32,)), dma((2, 8)), dma((2, SLOTS)), dma((2, 2)), dma((9,)), dma((4, 2)), dma((2,)), dma((2,)),
            dma((3,)), dma((2, 2)), dma((3,)), dma((2, 2)), dma((7,)), dma((4, 2)),
            dma((3, 2)), dma((3, 2)), dma((3,)), dma((3,)), dma((4, 2, 2)), dma((4, 2, 2)), dma((3, 7)), dma((3, 8)),
        ],
        compiler_params=pltpu.CompilerParams(
            collective_id=0, has_side_effects=True, vmem_limit_bytes=62 * MIB
        ),
    )(
        rows_of(hidden_in), rows_of(cotangent), norm_gain.reshape(1, D),
        w_query, w_key, w_value, w_out, jnp.asarray(cosine), jnp.asarray(sine), jnp.asarray(bias),
    )
    share = D // 128
    gain_share = lax.dynamic_slice_in_dim(gain_total.reshape(128), lax.rem(lax.axis_index("tensor"), 2) * share, share, 0)
    return (as_given(layer_out), as_given(input_grad)) + results(
        (query_share, key_share, value_share, out_share)
    ) + (gain_share,)


def solution(mesh):
    return jax.shard_map(
        shards,
        mesh=mesh,
        in_specs=(
            P("dp", "tensor", None), P(), P(None, "tensor"), P(None, "tensor"), P(None, "tensor"),
            P("tensor", None), P("dp", "tensor", None),
        ),
        out_specs=(
            P("dp", "tensor", None), P("dp", "tensor", None), P("dp", "tensor"), P("dp", "tensor"),
            P("dp", "tensor"), P("tensor", "dp"), P(("dp", "tensor")),
        ),
        check_vma=False,
    )
```

```python
import jax
import jax.numpy as jnp
import numpy as np
from jax import lax
from jax.experimental import pallas as pl
from jax.experimental.pallas import tpu as pltpu
from jax.sharding import PartitionSpec as P

HD = 128
EPS = 1e-05
ROPE_BASE = 10000.0
BF, F32 = jnp.bfloat16, jnp.float32
SLOTS, ROWS, D = 8, 24, 8192
PAIR, HALF = 2 * ROWS, D // 2
TOK = SLOTS * ROWS
SEQ_ROWS = 12
HEADS = 4
QC, KC = 512, 128
PIECES, PIECE, SLICE = 5, 256, 512
SCALE = HD ** (-0.5)
MESH_ID = pl.DeviceIdType.MESH
MIB = 1024 * 1024


def place():
    dp, tensor = lax.axis_index("dp"), lax.axis_index("tensor")
    core, chip = lax.rem(dp, 2), dp // 2
    z, xh = lax.rem(chip, 4), chip // 4
    y, xl = tensor // 2, lax.rem(tensor, 2)
    here = dict(z=z, xh=xh, core=core, y=y, xl=xl, dp=dp, tensor=tensor)

    def along_z(at, cross=0):
        return ((xh * 4 + at) * 2 + lax.rem(core + cross, 2), tensor)

    def along_y(at):
        return (dp, at * 2 + xl)

    here["z_up"] = along_z(lax.rem(z + 1, 4))
    here["z_down"] = along_z(lax.rem(z + 3, 4))
    here["z_up_cross"] = along_z(lax.rem(z + 1, 4), 1)
    here["z_down_cross"] = along_z(lax.rem(z + 3, 4), 1)
    here["pass_from"] = lax.rem(z + 3 + 2 * core, 4)
    here["pass_to"] = along_z(lax.rem(z + 1 + 2 * core, 4))
    here["y_up"] = along_y(lax.rem(y + 1, 4))
    here["y_down"] = along_y(lax.rem(y + 3, 4))
    here["x_lo"] = (dp, y * 2 + 1 - xl)
    here["x_hi"] = (((1 - xh) * 4 + z) * 2 + core, tensor)
    here["x_hi_cross"] = (((1 - xh) * 4 + z) * 2 + 1 - core, tensor)
    here["sibling"] = (chip * 2 + 1 - core, tensor)
    here["chip"] = chip
    here["tensor_peers"] = [(dp, lax.rem(tensor + i, 8)) for i in range(1, 8)]
    here["chip_peers"] = [(lax.rem(chip + i, 8) * 2 + core, tensor) for i in range(1, 8)]
    return here


def greet(devices):
    barrier = pltpu.get_barrier_semaphore()
    for device in devices:
        pl.semaphore_signal(barrier, inc=1, device_id=device, device_id_type=MESH_ID)
    pl.semaphore_wait(barrier, len(devices))


def remote(src, dst, send, recv, device):
    return pltpu.make_async_remote_copy(
        src_ref=src, dst_ref=dst, send_sem=send, recv_sem=recv, device_id=device, device_id_type=MESH_ID
    )


def dot(a, b, ca=1, cb=0):
    return lax.dot_general(a, b, (((ca,), (cb,)), ((), ())), preferred_element_type=F32)


def cols(at, width=SLICE):
    return pl.ds(pl.multiple_of(at * width, width), width)


def layer_kernel(
    hidden, cot, gain, w_query, w_key, w_value, w_out, cosine, sine, bias,
    layer_hbm, input_grad, query_hbm, key_hbm, value_hbm, out_hbm, gain_out,
    layer_out, query_share, key_share, value_share, out_share,
    wq, wkv, wo, rows_n, rows_c, rows_g, flat_n, raw_c, got_n, got_c, passed, mixed, grads,
    t_far_r, t_side_r, t_near_r, t_pair_r, far_r, side_r, near_r, pair_r,
    gain_own, gain_t, gain_c, gain_s, query_acc, kv_acc, query_rot, key_rot, values, grad_mixed, probs,
    inverse,
    out_sems, w_sems, wo_sems, a_send, a_recv, f_recv, s_send, s_recv, p_recv, own_sems, c_send, c_recv, h_send, h_recv, m_send, m_recv,
    d_send, d_recv, j_send, j_recv, t_send, t_recv, g_send, g_recv,
):
    here = place()
    y, xl, z, xh, core = here["y"], here["xl"], here["z"], here["xh"], here["core"]
    y_up, y_down, y_far = lax.rem(y + 1, 4), lax.rem(y + 3, 4), lax.rem(y + 2, 4)
    z_up, z_down, z_far = lax.rem(z + 1, 4), lax.rem(z + 3, 4), lax.rem(z + 2, 4)
    own, mate = here["tensor"], y * 2 + 1 - xl
    toward = ((here["y_up"], y_up), (here["y_down"], y_down))
    toward_z = ((here["z_up"], z_up), (here["z_down"], z_down))
    rows, sums = (rows_n, rows_c), (rows_n, rows_g)

    loads = (
        pltpu.make_async_copy(w_query, wq, w_sems.at[0]),
        pltpu.make_async_copy(w_key, wkv.at[:, pl.ds(0, KC)], w_sems.at[1]),
        pltpu.make_async_copy(w_value, wkv.at[:, pl.ds(KC, KC)], w_sems.at[2]),
    )

    def load_out(b):
        half, block = b // 16, lax.rem(b, 16)
        return pltpu.make_async_copy(w_out.at[cols(half, PIECE), cols(block)], wo.at[b], wo_sems.at[b])

    for copy in loads:
        copy.start()

    @pl.loop(0, 32)
    def _(b):
        load_out(b).start()

    def leaving(number):
        src, dst = (
            (out_share, out_hbm), (layer_out, layer_hbm), (query_share, query_hbm), (key_share, key_hbm),
            (value_share, value_hbm),
        )[number]
        return pltpu.make_async_copy(src, dst, out_sems.at[number])

    def leave(number):
        leaving(number).start()

    def mine(ref, at):
        return ref[:, :, at].astype(F32).reshape(ROWS, SLICE)

    def give(ref, at, block):
        ref[:, :, at] = block.reshape(SEQ_ROWS, 2, SLICE).astype(BF)

    def cot_block(i, zh):
        return 2 * ((i // 4) * 4 + 2 * zh + lax.rem(i, 2)) + lax.rem(i // 2, 2)

    def square(i, total):
        block = mine(hidden, cols(i))
        return total + jnp.sum(block * block, axis=1, keepdims=True)

    mean = lax.fori_loop(0, 16, square, jnp.zeros((ROWS, 1), F32)) / D
    inverse[...] = jnp.broadcast_to(lax.rsqrt(mean + EPS), (ROWS, 128))

    @pl.loop(0, 8)
    def _(k):
        scale = inverse[:, :1]
        normed = [
            mine(hidden, cols(2 * k + p)) * scale * gain[:, cols(2 * k + p)] for p in range(2)
        ]
        rows_n[own, :, cols(k)] = jnp.concatenate(normed, axis=0).astype(BF)
        rows_c[own, :, cols(k)] = jnp.concatenate(
            [mine(cot, cols(cot_block(k, zh))) for zh in range(2)], axis=0
        ).astype(BF)

    greet(
        here["tensor_peers"] + here["chip_peers"]
        + [here[name] for name in ("z_up_cross", "z_down_cross", "x_hi_cross", "sibling")]
    )

    pushed = ([], [])

    def push(a, number, slot, device):
        copy = remote(rows[a].at[slot], rows[a].at[slot], a_send.at[a, number], a_recv.at[a, slot], device)
        copy.start()
        pushed[a].append(copy)

    def landed(a, slot):
        remote(rows[a].at[slot], rows[a].at[slot], a_send.at[a, 0], a_recv.at[a, slot], here["x_lo"]).wait_recv()

    def push_over(a):
        push(a, 0, own, here["x_lo"])

    def push_along(a):
        push(a, 1, own, here["y_up"])
        push(a, 2, own, here["y_down"])

    def push_mate(a):
        landed(a, mate)
        push(a, 3, mate, here["y_up"])
        push(a, 4, mate, here["y_down"])

    halves = (pl.ds(0, HALF // 2), pl.ds(HALF // 2, HALF // 2))

    def far_copy(a, way):
        slot = (y_down, y_up)[way] * 2 + xl
        ref = rows[a].at[slot, :, halves[way]]
        return remote(ref, ref, a_send.at[a, 5 + way], f_recv.at[a, way], toward[way][0])

    def push_far(a):
        if a:
            landed(a, y_down * 2)
            push(a, 5, y_down * 2, here["y_up"])
            share(y_down * 2)
            landed(a, y_up * 2 + 1)
            push(a, 6, y_up * 2 + 1, here["y_down"])
            share(y_up * 2 + 1)
            return
        for way in range(2):
            landed(a, (y_down, y_up)[way] * 2 + xl)
            copy = far_copy(a, way)
            copy.start()
            pushed[a].append(copy)

    def push_last(a):
        slot = y_far * 2 + xl
        for way in range(2):
            ref = rows[a].at[slot, :, halves[way]]
            remote(ref, ref, a_send.at[a, 0], f_recv.at[a, way], here["x_lo"]).wait_recv()
        push(a, 7, slot, here["x_lo"])

    def rest(a):
        if a:
            for slot in (y_down * 2 + 1, y_up * 2, y_far * 2, y_far * 2 + 1):
                landed(a, slot)
                share(slot)
            return
        landed(a, y_down * 2 + 1 - xl)
        landed(a, y_up * 2 + 1 - xl)
        landed(a, y_far * 2 + 1 - xl)

    def flatten(a, k):
        chunks = [rows[a][slot, :, cols(k)].astype(F32) for slot in range(SLOTS)]
        return whole(chunks)

    def whole(chunks):
        return [
            jnp.concatenate([c[p * ROWS : (p + 1) * ROWS] for c in chunks], axis=0).astype(BF) for p in range(2)
        ]

    def slice_copy(number):
        cross = 1 - core
        src, dst, recv, device = (
            (flat_n.at[core, z_far], passed.at[0], p_recv.at[0], "z_up"),
            (flat_n.at[cross, z_far], passed.at[1], p_recv.at[1], "z_down"),
            (flat_n.at[core, z_up], got_n.at[z, core], s_recv.at[z, core], "z_up"),
            (flat_n.at[core, z_down], got_n.at[z, core], s_recv.at[z, core], "z_down"),
            (flat_n.at[cross, z_up], got_n.at[z, core], s_recv.at[z, core], "z_up_cross"),
            (flat_n.at[cross, z_down], got_n.at[z, core], s_recv.at[z, core], "z_down_cross"),
            (flat_n.at[cross, z], got_n.at[z, core], s_recv.at[z, core], "sibling"),
            (passed.at[0], got_n.at[z_down, core], s_recv.at[z_down, core], "z_up"),
            (passed.at[1], got_n.at[z_up, core], s_recv.at[z_up, core], "z_down_cross"),
        )[number]
        return remote(src, dst, s_send.at[number], recv, here[device])

    def own_slice():
        return pltpu.make_async_copy(flat_n.at[core, z], got_n.at[z, core], own_sems.at[0])

    def slices_pass():
        for number in range(2):
            slice_copy(number).wait_recv()
            slice_copy(7 + number).start()

    def slices_wait():
        own_slice().wait()
        for at, cross in ((0, 1), (1, 0), (1, 1), (2, 0), (2, 1), (3, 0), (3, 1)):
            zs, cs = lax.rem(z + at, 4), lax.rem(core + cross, 2)
            ref = got_n.at[zs, cs]
            remote(ref, ref, s_send.at[0], s_recv.at[zs, cs], here["sibling"]).wait_recv()

    def cot_copy(number, slot):
        side, parity, device = (
            (xh, 1 - core, "sibling"), (1 - xh, core, "x_hi"), (1 - xh, 1 - core, "x_hi_cross"),
        )[number]
        src = rows_c.at[slot, :, cols(side * 2 + parity, 2 * SLICE)]
        return remote(
            src, raw_c.at[number, slot], c_send.at[slot, number], c_recv.at[number, slot], here[device]
        )

    def share(slot):
        for number in (1, 2, 0):
            cot_copy(number, slot).start()

    def mix_copy(number):
        device = ("x_hi", "x_hi_cross", "sibling")[number]
        ref = mixed.at[xh, core]
        return remote(ref, ref, h_send.at[number], h_recv.at[xh, core], here[device])

    def cross_wait():
        for number, (xs, cs) in enumerate(((xh, 1 - core), (1 - xh, core), (1 - xh, 1 - core))):
            ref = mixed.at[xs, cs]
            remote(ref, ref, h_send.at[0], h_recv.at[xs, cs], here["sibling"]).wait_recv()
            for slot in range(SLOTS):
                ref = raw_c.at[number, slot]
                remote(ref, ref, c_send.at[slot, 0], c_recv.at[number, slot], here["sibling"]).wait_recv()
            for zl in range(2):
                chunks = [raw_c[number, slot, :, zl * SLICE : (zl + 1) * SLICE].astype(F32) for slot in range(SLOTS)]
                for zh, block in enumerate(whole(chunks)):
                    got_c[xs, cs, 2 * zh + zl] = block

    def columns_copy(number):
        at, device = (
            (z, "sibling"), (z, "z_up"), (z, "z_down"), (z_down, "sibling"), (z_up, "sibling"),
            (here["pass_from"], "pass_to"), (z_far, "sibling"),
        )[number]
        ref = grads.at[at, core]
        return remote(ref, ref, m_send.at[number], m_recv.at[at, core], here[device])

    def columns_got(zs, cs):
        ref = grads.at[zs, cs]
        remote(ref, ref, m_send.at[0], m_recv.at[zs, cs], here["sibling"]).wait_recv()

    def columns_start():
        for number in (1, 2, 0):
            columns_copy(number).start()

    def columns_pass():
        columns_got(z_down, core)
        columns_got(z_up, core)
        for number in (5, 3, 4):
            columns_copy(number).start()

    def columns_last():
        columns_got(z_far, core)
        columns_copy(6).start()

    def columns_wait():
        for zs in range(4):
            columns_got(zs, 1 - core)

    push_over(0)
    push_along(0)
    push_mate(0)
    push_far(0)
    push_over(1)
    push_last(0)
    push_along(1)
    push_mate(1)
    rest(0)
    share(own)
    share(mate)

    query_acc[...] = jnp.zeros_like(query_acc)
    kv_acc[...] = jnp.zeros_like(kv_acc)
    for copy in loads:
        copy.wait()

    for step, at in enumerate((z_far, z_up, z_down, z)):
        @pl.loop(0, 2)
        def _(side, at=at):
            k = side * 4 + at
            for p, block in enumerate(flatten(0, k)):
                flat_n[p, at, side] = block
                query_acc[...] += dot(block, wq[cols(2 * k + p), :])
                kv_acc[...] += dot(block, wkv[cols(2 * k + p), :])

        for number in ((0, 1), (2, 4), (3, 5), (6,))[step]:
            slice_copy(number).start()
    own_slice().start()

    def rotated(u):
        return u * cosine[...] + pltpu.roll(u, HD // 2, 1) * sine[...]

    def unrotated(g):
        return g * cosine[...] - pltpu.roll(g, HD // 2, 1) * sine[...]

    def head(h):
        return slice(h * HD, (h + 1) * HD)

    key_rot[...] = rotated(kv_acc[:, :HD]).astype(BF)
    values[...] = kv_acc[:, HD:].astype(BF)
    for h in range(HEADS):
        query_rot[:, head(h)] = rotated(query_acc[:, head(h)]).astype(BF)
    for h in range(HEADS):
        logits = dot(query_rot[:, head(h)], key_rot[...], 1, 1) * SCALE + bias[...]
        powers = jnp.exp(logits - jnp.max(logits, axis=1, keepdims=True))
        prob = powers / jnp.sum(powers, axis=1, keepdims=True)
        probs[h] = prob
        mixed[xh, core, :, head(h)] = dot(prob.astype(BF), values[...]).astype(BF)
    for number in range(3):
        mix_copy(number).start()

    @pl.loop(0, 32)
    def _(b):
        load_out(b).wait()

    for copy in pushed[0]:
        copy.wait_send()

    def to_chunks(a, k, blocks):
        for slot in range(SLOTS):
            sums[a][slot, :, cols(k)] = jnp.concatenate(
                [b[slot * ROWS : (slot + 1) * ROWS] for b in blocks], axis=0
            ).astype(BF)

    @pl.loop(0, 8)
    def _(k):
        to_chunks(0, k, [
            dot(mixed[xh, core, :, :PIECE], wo[2 * k + p]) + dot(mixed[xh, core, :, PIECE:], wo[16 + 2 * k + p]) for p in range(2)
        ])

    def t_copy(kind, a, way):
        device, at = toward[way]
        slot = (y_far * 2 + way, at * 2 + 1 - way, at * 2 + way)[kind]
        dst = (t_far_r, t_side_r, t_near_r)[kind].at[a, way]
        return remote(sums[a].at[slot], dst, t_send.at[kind, a, way], t_recv.at[kind, a, way], device)

    def t_start(a):
        for kind in range(2):
            for way in range(2):
                t_copy(kind, a, way).start()

    def t_relay(a):
        for way in range(2):
            t_copy(0, a, way).wait()
            slot = toward[way][1] * 2 + way

            @pl.loop(0, 8)
            def _(k, way=way, slot=slot):
                sums[a][slot, :, cols(k)] = (
                    sums[a][slot, :, cols(k)].astype(F32) + t_far_r[a, way, :, cols(k)].astype(F32)
                ).astype(BF)

            t_copy(2, a, way).start()

    def t_total(a, side, k):
        return (
            sums[a][y * 2 + side, :, cols(k)].astype(F32)
            + t_side_r[a, 1 - side, :, cols(k)].astype(F32)
            + t_near_r[a, side, :, cols(k)].astype(F32)
        )

    def t_pair(a):
        return remote(sums[a].at[mate], t_pair_r.at[a], t_send.at[3, a, 0], t_recv.at[3, a, 0], here["x_lo"])

    def t_settle(a):
        for way in range(2):
            t_copy(1, a, way).wait()
            t_copy(2, a, way).wait()

        @pl.loop(0, 8)
        def _(k):
            sums[a][mate, :, cols(k)] = t_total(a, 1 - xl, k).astype(BF)

        t_pair(a).start()

    push_far(1)
    t_start(0)
    slices_pass()
    rest(1)

    query_acc[...] = jnp.zeros_like(query_acc)

    @pl.loop(0, 8)
    def _(i):
        for zh, block in enumerate(flatten(1, i)):
            at = cot_block(i, zh)
            for half in range(2):
                query_acc[:, half * PIECE : (half + 1) * PIECE] += dot(block, wo[half * 16 + at], 1, 1)

    for zl in range(2):
        for zh, block in enumerate(flatten(1, (xh * 2 + core) * 2 + zl)):
            got_c[xh, core, 2 * zh + zl] = block
    grad_mixed[...] = query_acc[...].astype(BF)

    def joint(p, side):
        total = jnp.zeros((PIECE, SLICE), F32)
        for zs in range(4):
            for cs in range(2):
                total += dot(grads[zs, cs, :, p * PIECE : (p + 1) * PIECE], got_n[zs, cs, side], 0, 0)
        return total

    def joint_pair(p):
        return remote(wo.at[p], pair_r.at[p], j_send.at[p], j_recv.at[p], here["x_hi"])

    def outer(p, at):
        total = jnp.zeros((PIECE, SLICE), F32)
        for xs in range(2):
            for cs in range(2):
                total += dot(mixed[xs, cs, :, p * PIECE : (p + 1) * PIECE], got_c[xs, cs, at], 0, 0)
        return total

    def d_copy(kind, way):
        dst = (far_r, side_r, near_r)[kind].at[way]
        return remote(wo.at[3 + kind * 2 + way], dst, d_send.at[kind, way], d_recv.at[kind, way], toward_z[way][0])

    dkey = jnp.zeros((TOK, HD), F32)
    dvalues = jnp.zeros((TOK, HD), F32)
    for h in range(HEADS):
        prob = probs[h]
        grad = grad_mixed[:, head(h)]
        dvalues += dot(prob.astype(BF), grad, 0, 0)
        prob_grad = dot(grad, values[...], 1, 1)
        row_delta = jnp.sum(prob * prob_grad, axis=1, keepdims=True)
        score_grad = (prob * (prob_grad - row_delta) * SCALE).astype(BF)
        grads[z, core, :, head(h)] = unrotated(dot(score_grad, key_rot[...])).astype(BF)
        dkey += dot(score_grad, query_rot[:, head(h)], 0, 0)
    grads[z, core, :, QC : QC + HD] = unrotated(dkey).astype(BF)
    grads[z, core, :, QC + HD :] = dvalues.astype(BF)
    columns_start()
    t_relay(0)


    @pl.loop(0, 8)
    def _(k):
        blocks = []
        for p in range(2):
            at = 2 * k + p
            block = dot(grads[z, core, :, :QC], wq[cols(at), :], 1, 1)
            block += dot(grads[z, core, :, QC:], wkv[cols(at), :], 1, 1)
            blocks.append(block)
            terms = block.astype(BF).astype(F32) * flat_n[p, lax.rem(k, 4), k // 4].astype(F32)
            term = jnp.sum(terms, axis=0, keepdims=True) / gain[:, cols(at)]
            for quarter in range(4):
                gain_own[quarter, pl.ds(at, 1), :] = term[:, quarter * 128 : (quarter + 1) * 128]
        to_chunks(1, k, blocks)

    def gain_over(number):
        at = lax.rem(own + 1 + number, 8) // 2
        return remote(
            gain_own.at[at], gain_t.at[own], g_send.at[0, number], g_recv.at[0, own], here["tensor_peers"][number]
        )

    def gain_sibling():
        return remote(gain_s.at[0], gain_s.at[1], g_send.at[1, 0], g_recv.at[1, 0], here["sibling"])

    def gain_chips(number):
        return remote(
            gain_s.at[2], gain_c.at[here["chip"]], g_send.at[2, number], g_recv.at[2, here["chip"]],
            here["chip_peers"][number],
        )

    def gain_sum(level, ref, mine, value):
        ref[mine] = value
        for i in range(1, 8):
            at = lax.rem(mine + i, 8)
            remote(ref.at[at], ref.at[at], g_send.at[level, 0], g_recv.at[level, at], here["sibling"]).wait_recv()
        total = ref[0]
        for i in range(1, 8):
            total = total + ref[i]
        return total

    for number in range(7):
        gain_over(number).start()
    t_start(1)
    cross_wait()
    columns_pass()
    for way in range(2):
        wo[3 + way] = outer(way, z_far).astype(BF)
        d_copy(0, way).start()
    for way in range(2):
        wo[5 + way] = outer(1 - way, toward_z[way][1]).astype(BF)
        d_copy(1, way).start()
    t_settle(0)
    columns_last()
    t_relay(1)
    slices_wait()
    columns_wait()
    for p in range(3):
        wo[p] = joint(p, 1 - xh).astype(BF)
        joint_pair(p).start()
    for way in range(2):
        block = outer(way, toward_z[way][1])
        d_copy(0, way).wait()
        wo[7 + way] = (block + far_r[way].astype(F32)).astype(BF)
        d_copy(2, way).start()
    gain_s[0] = gain_sum(0, gain_t, own, gain_own[y])
    gain_sibling().start()
    gain_sibling().wait()
    gain_s[2] = gain_s[0] + gain_s[1]
    for number in range(7):
        gain_chips(number).start()
    t_settle(1)
    for p in range(3):
        total = joint(p, xh).T
        if p < 2:
            query_share[:, p * PIECE : (p + 1) * PIECE] = total
        else:
            key_share[...] = total[:, :KC]
            value_share[...] = total[:, KC:]
    for p in range(2):
        out_share[p * PIECE : (p + 1) * PIECE, :] = outer(p, z)
    for p in range(2):
        d_copy(1, 1 - p).wait()
        d_copy(2, p).wait()
        out_share[p * PIECE : (p + 1) * PIECE, :] += side_r[1 - p].astype(F32) + near_r[p].astype(F32)
    leave(0)
    t_pair(0).wait()

    @pl.loop(0, 8)
    def _(k):
        total = t_total(0, xl, k) + t_pair_r[0, :, cols(k)].astype(F32)
        for p in range(2):
            at = cols(2 * k + p)
            give(layer_out, at, mine(hidden, at) + total[p * ROWS : (p + 1) * ROWS])

    leave(1)
    for p in range(3):
        joint_pair(p).wait()
        total = pair_r[p].astype(F32).T
        if p < 2:
            query_share[:, p * PIECE : (p + 1) * PIECE] += total
        else:
            key_share[...] += total[:, :KC]
            value_share[...] += total[:, KC:]
    for number in range(2, 5):
        leave(number)
    t_pair(1).wait()
    scale = inverse[:, :1]

    def weigh(k, total):
        block = t_total(1, xl, k) + t_pair_r[1, :, cols(k)].astype(F32)
        for p in range(2):
            at = cols(2 * k + p)
            scaled = mine(hidden, at) * scale
            weighted = block[p * ROWS : (p + 1) * ROWS] * gain[:, at]
            total = total + jnp.sum(weighted * scaled, axis=1, keepdims=True)
        return total

    mean = lax.fori_loop(0, 8, weigh, jnp.zeros((ROWS, 1), F32)) / D

    @pl.loop(0, 8)
    def _(k):
        block = t_total(1, xl, k) + t_pair_r[1, :, cols(k)].astype(F32)
        for p in range(2):
            at = cols(2 * k + p)
            scaled = mine(hidden, at) * scale
            weighted = block[p * ROWS : (p + 1) * ROWS] * gain[:, at]
            give(input_grad, at, mine(cot, at) + scale * (weighted - scaled * mean))

    gain_s[3] = gain_sum(2, gain_c, here["chip"], gain_s[2])
    gain_out[...] = gain_s[3, pl.ds(here["dp"], 1), :]
    for copy in pushed[1]:
        copy.wait_send()
    for slot in range(SLOTS):
        for number in range(3):
            cot_copy(number, slot).wait_send()
    for number in range(5):
        leaving(number).wait()
    for number in range(7):
        gain_over(number).wait_send()
        gain_chips(number).wait_send()
    for number in range(9):
        slice_copy(number).wait_send()
    for number in range(7):
        columns_copy(number).wait_send()
    for number in range(3):
        mix_copy(number).wait_send()


def copy_kernel(*refs):
    count = len(refs) // 2
    for i in range(count):
        refs[count + i][...] = refs[i][...]


def results(arrays):
    at_vmem = pl.BlockSpec(memory_space=pltpu.VMEM)
    return pl.pallas_call(
        copy_kernel,
        out_shape=tuple(jax.ShapeDtypeStruct(a.shape, a.dtype) for a in arrays),
        in_specs=[at_vmem] * len(arrays),
        out_specs=tuple([at_vmem] * len(arrays)),
    )(*arrays)


def tables(own_len):
    token = np.arange(TOK)
    seq = token % 2
    pos = (token // ROWS) * own_len + token % ROWS // 2
    frequency = ROPE_BASE ** (-2.0 * np.arange(HD // 2) / HD)
    angles = pos[:, None] * frequency[None, :]
    cosine = np.concatenate([np.cos(angles), np.cos(angles)], axis=1).astype(np.float32)
    sine = np.concatenate([-np.sin(angles), np.sin(angles)], axis=1).astype(np.float32)
    allowed = (seq[:, None] == seq[None, :]) & (pos[:, None] >= pos[None, :])
    return cosine, sine, np.where(allowed, 0.0, -1e30).astype(np.float32)


def shards(hidden_in, norm_gain, w_query, w_key, w_value, w_out, cotangent):
    dma, vmem = pltpu.SemaphoreType.DMA, pltpu.VMEM
    chunk = (PAIR, HALF)
    block = (PIECE, SLICE)
    at_vmem = pl.BlockSpec(memory_space=pltpu.VMEM)
    at_any = pl.BlockSpec(memory_space=pl.ANY)
    shape = jax.ShapeDtypeStruct
    cosine, sine, bias = tables(SEQ_ROWS)
    own_shape = (SEQ_ROWS, 2, D)

    def rows_of(array):
        return array.transpose(1, 0, 2)

    def as_given(array):
        return array.transpose(1, 0, 2)

    layer_out, input_grad, query_share, key_share, value_share, out_share, gain_total = pl.pallas_call(
        layer_kernel,
        out_shape=(
            shape(own_shape, BF), shape(own_shape, BF), shape((SLICE, QC), F32), shape((SLICE, KC), F32),
            shape((SLICE, KC), F32), shape((QC, SLICE), F32), shape((1, 128), F32),
        ),
        in_specs=[at_vmem] * 3 + [at_any] * 4 + [at_vmem] * 3,
        out_specs=(at_any, at_vmem, at_any, at_any, at_any, at_any, at_vmem),
        scratch_shapes=[
            vmem((SEQ_ROWS, 2, D), BF), vmem((SLICE, QC), F32), vmem((SLICE, KC), F32), vmem((SLICE, KC), F32),
            vmem((QC, SLICE), F32),
            vmem((D, QC), BF), vmem((D, 2 * KC), BF), vmem((32,) + block, BF),
            vmem((SLOTS,) + chunk, BF), vmem((SLOTS,) + chunk, BF), vmem((SLOTS,) + chunk, BF),
            vmem((2, 4, 2, TOK, SLICE), BF), vmem((3, SLOTS, PAIR, 2 * SLICE), BF),
            vmem((4, 2, 2, TOK, SLICE), BF), vmem((2, 2, 4, TOK, SLICE), BF),
            vmem((2, 2, TOK, SLICE), BF), vmem((2, 2, TOK, QC), BF), vmem((4, 2, TOK, QC + 2 * KC), BF),
            vmem((2, 2) + chunk, BF), vmem((2, 2) + chunk, BF), vmem((2, 2) + chunk, BF), vmem((2,) + chunk, BF),
            vmem((2,) + block, BF), vmem((2,) + block, BF), vmem((2,) + block, BF), vmem((3,) + block, BF),
            vmem((4, 16, 128), F32), vmem((8, 16, 128), F32), vmem((8, 16, 128), F32), vmem((4, 16, 128), F32),
            vmem((TOK, QC), F32), vmem((TOK, 2 * KC), F32),
            vmem((TOK, QC), BF), vmem((TOK, HD), BF), vmem((TOK, HD), BF),
            vmem((TOK, QC), BF),
            vmem((HEADS, TOK, TOK), F32), vmem((ROWS, 128), F32),
            dma((5,)), dma((3,)), dma((32,)), dma((2, 8)), dma((2, SLOTS)), dma((2, 2)), dma((9,)), dma((4, 2)), dma((2,)), dma((2,)),
            dma((SLOTS, 3)), dma((3, SLOTS)), dma((3,)), dma((2, 2)), dma((7,)), dma((4, 2)),
            dma((3, 2)), dma((3, 2)), dma((3,)), dma((3,)), dma((4, 2, 2)), dma((4, 2, 2)), dma((3, 7)), dma((3, 8)),
        ],
        compiler_params=pltpu.CompilerParams(
            collective_id=0, has_side_effects=True, vmem_limit_bytes=62 * MIB
        ),
    )(
        rows_of(hidden_in), rows_of(cotangent), norm_gain.reshape(1, D),
        w_query, w_key, w_value, w_out, jnp.asarray(cosine), jnp.asarray(sine), jnp.asarray(bias),
    )
    share = D // 128
    gain_share = lax.dynamic_slice_in_dim(gain_total.reshape(128), lax.rem(lax.axis_index("tensor"), 2) * share, share, 0)
    layer_out, input_grad, *weight_shares = results(
        (layer_out, input_grad, query_share, key_share, value_share, out_share)
    )
    return (as_given(layer_out), as_given(input_grad), *weight_shares, gain_share)


def solution(mesh):
    return jax.shard_map(
        shards,
        mesh=mesh,
        in_specs=(
            P("dp", "tensor", None), P(), P(None, "tensor"), P(None, "tensor"), P(None, "tensor"),
            P("tensor", None), P("dp", "tensor", None),
        ),
        out_specs=(
            P("dp", "tensor", None), P("dp", "tensor", None), P("dp", "tensor"), P("dp", "tensor"),
            P("dp", "tensor"), P("tensor", "dp"), P(("dp", "tensor")),
        ),
        check_vma=False,
    )
```
